32 devices in a mesh: expgrp: 8 (over z, core), patch: 4 (over y, x).
Axes of the slice: x: 2, y: 2, z: 4, core: 2. Of those that a mesh axis runs over, the one named last changes fastest.
Arguments:
- image: float32 [2048, 1024], P(('expgrp', 'patch')), may hold values from -6 to 6
- variance: float32 [2048, 1024], P(('expgrp', 'patch')), may hold values from 0.25 to 4
- block_count: int32 [32, 4], P('expgrp'), may hold values from 0 to 2, as said below
- slot_start: int32 [32, 4], P('expgrp'), may hold values from 0 to 16, as said below
- psf_index: int32 [32], P('expgrp'), may hold values from 0 to 63
- coef_table: float32 [64, 3], replicated, may hold values from 0.1 to 1
Outputs:
- coadd: float32 [1024, 1024], P('patch')
The draws below stay inside these ranges and needn't reach their ends.
Inputs may be any that keep to these rules, and one draw needn't show every extreme that they name: Each row of block_count sums to 4. In each exposure group one patch owner, drawn per group, receives 2 blocks from every exposure of the group. slot_start + block_count <= 16 for every exposure and owner.
All inputs are finite; a program needn't handle non-finite values.
Results may differ from the reference program's by a relative error of at most 0.0001.
Values sent between devices are 32-bit elements; how exact they have to be, the bound alone decides.
A program may use at most 64 MiB of HBM per device.

```python
import math
import jax
import jax.numpy as jnp
from jax import lax

W = 1024
BLK = 16
CAP = 2
NB = 4
NS = 16
KH = 10
BASES = 3
NCOEF = 64
EXPOSURES = 32
TILE_ROWS = 2048
N_EXPGRP = 8
N_PATCH = 4


def margin_layout(key):
    base = jax.random.fold_in(key, 7)
    hot_key, order_key, slot_key = jax.random.split(base, 3)
    hottest = jax.random.randint(hot_key, (N_EXPGRP,), 0, N_PATCH).astype(jnp.int32)
    hot_each = jnp.repeat(hottest, N_PATCH)
    owner_of = (jnp.arange(N_PATCH * CAP) // CAP).astype(jnp.int32)
    order_keys = jax.random.split(order_key, EXPOSURES)
    scores = jax.vmap(lambda single: jax.random.permutation(single, N_PATCH * CAP))(order_keys).astype(jnp.int32)
    scores = scores + jnp.where(owner_of[None, :] == hot_each[:, None], N_PATCH * CAP, 0).astype(jnp.int32)
    ranking = jnp.argsort(scores, axis=1)
    chosen = owner_of[ranking[:, :NB - CAP]]
    owner_range = jnp.arange(N_PATCH).astype(jnp.int32)
    extra = jnp.sum((chosen[:, :, None] == owner_range[None, None, :]).astype(jnp.int32), axis=1)
    counts = extra + CAP * (owner_range[None, :] == hot_each[:, None]).astype(jnp.int32)
    starts = jax.random.randint(slot_key, (EXPOSURES, N_PATCH), 0, NS - counts + 1)
    return (counts.astype(jnp.int32), starts.astype(jnp.int32))


def draw_block_count(key, part):
    return margin_layout(key)[0]


def draw_slot_start(key, part):
    return margin_layout(key)[1]


def plant(values, rng, least, top_value):
    longest = values.shape.index(max(values.shape))
    spots = []
    for shift in (0, 1):
        where = [jax.random.randint(jax.random.fold_in(rng, axis), (), 0, length) for axis, length in enumerate(values.shape)]
        where[longest] = (where[longest] + shift) % values.shape[longest]
        spots.append(tuple(where))
    return values.at[spots[0]].set(least).at[spots[1]].set(top_value)


def block_levels(key, dims, cuts, low, top_value):
    level, own = 1.0, jax.random.fold_in(key, 6)
    for axis_at, blocks in cuts:
        steps = jnp.exp(jax.random.uniform(jax.random.fold_in(own, axis_at), (blocks,), jnp.float32, low / len(cuts), top_value / len(cuts)))
        level = level * jnp.repeat(steps, dims[axis_at] // blocks).reshape([-1 if axis == axis_at else 1 for axis in range(len(dims))])
    return level


def noise(own_key, extent, spread, most, shards=(), kind=jnp.bfloat16):
    array = spread * jax.random.normal(own_key, extent, jnp.float32)
    if shards:
        array = array * block_levels(own_key, extent, shards, -0.22, 0.18)
    return jnp.clip(array, -most, most).astype(kind)


def setup_inputs(seed: int = 0) -> dict:
    seeds = jax.random.split(jax.random.key(seed), 7)
    image = noise(seeds[0], (TILE_ROWS, W), 1.0, 6.0, ((0, 32),), jnp.float32)
    variance = jnp.clip(jnp.exp(math.log(4.0) - 2.7725887 * jax.random.uniform(seeds[1], (TILE_ROWS, W), jnp.float32) ** block_levels(seeds[1], (TILE_ROWS, W), ((0, 32),), -0.2, 0.2)), 0.25, 4.0)
    block_count = draw_block_count(jax.random.fold_in(seeds[6], 71), 0)
    slot_start = draw_slot_start(jax.random.fold_in(seeds[6], 71), 0)
    psf_index = plant(jax.random.randint(seeds[4], (EXPOSURES,), 0, NCOEF), jax.random.fold_in(seeds[4], 1), 0, NCOEF - 1).astype(jnp.int32)
    coef_table = jnp.clip(jax.random.uniform(seeds[5], (NCOEF, BASES), jnp.float32, 0.1, 1.0), 0.1, 1.0)
    return {"image": image, "variance": variance, "block_count": block_count, "slot_start": slot_start, "psf_index": psf_index, "coef_table": coef_table}


SIGMAS = (0.75, 1.5, 3.0)


def profile(offsets, deviation):
    offset_range = jnp.arange(-KH, KH + 1).astype(jnp.float32)
    total = jnp.sum(jnp.exp(-offset_range * offset_range / (2.0 * deviation * deviation)))
    spacing = offsets.astype(jnp.float32)
    return jnp.where(jnp.abs(offsets) <= KH, jnp.exp(-spacing * spacing / (2.0 * deviation * deviation)) / total, jnp.float32(0.0))


def smoothed(blocks, deviation):
    padded = jnp.pad(blocks, ((0, 0), (0, 0), (KH, KH)))
    across = jnp.zeros_like(blocks)
    for offset in range(-KH, KH + 1):
        factor = profile(jnp.asarray(offset, dtype=jnp.int32), deviation)
        across = across + factor * padded[:, :, KH + offset:KH + offset + W]
    padded = jnp.pad(across, ((0, 0), (KH, KH), (0, 0)))
    result = jnp.zeros_like(blocks)
    for offset in range(-KH, KH + 1):
        factor = profile(jnp.asarray(offset, dtype=jnp.int32), deviation)
        result = result + factor * padded[:, KH + offset:KH + offset + BLK, :]
    return result


def reference(image, variance, block_count, slot_start, psf_index, coef_table):
    exposures = block_count.shape[0]
    image_blocks = image.reshape(exposures, NB, BLK, W)
    scale_blocks = variance.reshape(exposures, NB, BLK, W)
    lookup = (jnp.arange(NCOEF).astype(jnp.int32)[None, :] == psf_index.astype(jnp.int32)[:, None]).astype(jnp.float32)
    mixing = jnp.sum(lookup[:, :, None] * coef_table[None, :, :], axis=1)

    def one_exposure(inputs):
        blocks, scales, weights_row = inputs
        matched = jnp.zeros_like(blocks)
        for basis in range(len(SIGMAS)):
            matched = matched + weights_row[basis] * smoothed(blocks, SIGMAS[basis])
        weight = 1.0 / scales
        return weight * matched, weight

    flux, weight = lax.map(one_exposure, (image_blocks, scale_blocks, mixing))
    counts = block_count.astype(jnp.int32)
    run_ends = jnp.cumsum(counts, axis=1).astype(jnp.int32)
    firsts = (run_ends - counts).astype(jnp.int32)
    block_index = jnp.arange(NB).astype(jnp.int32)
    owner = jnp.sum((run_ends[:, None, :] <= block_index[None, :, None]).astype(jnp.int32), axis=2).astype(jnp.int32)
    first_of = jnp.take_along_axis(firsts, owner, axis=1).astype(jnp.int32)
    slot_of = jnp.take_along_axis(slot_start.astype(jnp.int32), owner, axis=1).astype(jnp.int32)
    destination = (owner * NS + slot_of + block_index[None, :] - first_of).astype(jnp.int32).reshape(-1)
    flux_sum = jax.ops.segment_sum(flux.reshape(exposures * NB, BLK * W), destination, num_segments=N_PATCH * NS)
    weight_sum = jax.ops.segment_sum(weight.reshape(exposures * NB, BLK * W), destination, num_segments=N_PATCH * NS)
    coadd = flux_sum / jnp.maximum(weight_sum, 1.0)
    return coadd.reshape(N_PATCH * NS * BLK, W)
```

```python
import functools
import math

import jax
import jax.numpy as jnp
import numpy as np
from jax import lax
from jax.experimental import pallas as pl
from jax.experimental.pallas import tpu as pltpu
from jax.sharding import PartitionSpec as P

BLK = 16
CAP = 2
NS = 16
KH = 10
NB = 4
LANES = 128
SIDE = 64


SIGMAS = (0.75, 1.5, 3.0)
BASES = len(SIGMAS)
highest = lax.Precision.HIGHEST
MESH = pl.DeviceIdType.MESH


def np_profile(offsets, deviation):
    every = np.arange(-KH, KH + 1, dtype=np.float64)
    total = np.sum(np.exp(-every * every / (2.0 * deviation * deviation)))
    spacing = offsets.astype(np.float64)
    return np.where(
        np.abs(offsets) <= KH, np.exp(-spacing * spacing / (2.0 * deviation * deviation)) / total, 0.0
    ).astype(np.float32)


def np_row_table():
    row = np.arange(BLK * NB)
    r, n = row // NB, row % NB
    m, k = row // BLK, row % BLK
    same = (n[:, None] == m[None, :]).astype(np.float32)
    return np.concatenate([same * np_profile(k[None, :] - r[:, None], s) for s in SIGMAS], axis=0)


def np_column_table():
    i = np.arange(LANES + 2 * SIDE)[:, None]
    c = np.arange(LANES)[None, :]
    whole = np.concatenate([np_profile(i - SIDE - c, s) for s in SIGMAS], axis=0)
    high = whole.astype(jnp.bfloat16)
    low = (whole - high.astype(np.float32)).astype(jnp.bfloat16)
    return np.concatenate([high, low], axis=1)


def halves(x):
    high = x.astype(jnp.bfloat16)
    return high, (x - high.astype(jnp.float32)).astype(jnp.bfloat16)


def dot(a, b):
    return jnp.dot(a, b, preferred_element_type=jnp.float32)


def kernel(groups, owners, *refs):
    inputs, out, stage = refs[:8], refs[8], refs[9:17]
    (xpad, vbuf, wbuf, fbuf, dsrc, warr, farr, rd, cbuf,
     sw, qw, sf, qf, sd, qd, so, qo, sx, qx, above, local, fetch) = refs[17:]
    loads = [pltpu.make_async_copy(a, b, fetch.at[n]) for n, (a, b) in enumerate(zip(inputs, stage))]
    for n in (1, 2, 3, 0, 4, 5, 6, 7):
        loads[n].start()
    img, var, count, start, psf, coef, rows_t, cols_t = stage
    g, p = lax.axis_index("expgrp"), lax.axis_index("patch")
    devices = groups * owners
    me = g * owners + p
    columns = img.shape[1]
    tiles = columns // LANES
    chips = groups // 2
    plane = 2 * owners
    z, core = g // 2, g % 2
    low = plane * (z + 1)

    def place_of(k):
        return (k // owners, lax.rem(k, owners))

    barrier = pltpu.get_barrier_semaphore()

    @pl.loop(1, devices - plane * z)
    def _(s):
        k = plane * z + lax.rem(me - plane * z + s, devices - plane * z)
        pl.semaphore_signal(barrier, inc=1, device_id=place_of(k), device_id_type=MESH)

    loads[2].wait()
    loads[3].wait()
    lane = lax.broadcasted_iota(jnp.int32, (1, LANES), 1)
    place = jnp.zeros((1, LANES), jnp.int32)
    block = lax.rem(lane, NB)
    for e in range(owners):
        first = jnp.int32(0)
        for q in range(owners):
            n_here = count[e, q]
            base = q * NS + start[e, q] - first
            inside = (lane // 8 == e) & (block >= first) & (block < first + n_here)
            place = jnp.where(inside, base + block, place)
            first = first + n_here
    dsrc[0] = place
    rd[g] = place
    loads[1].wait()

    for t in range(tiles):
        vbuf[t] = 1.0 / var[:, t * LANES:(t + 1) * LANES]
        for r in range(BLK):
            h, i = r // 8, (r // 2) % 4
            wbuf[t * owners + i, h, (r % 2) * NB:(r % 2) * NB + NB, :] = vbuf[t, pl.ds(r, NB, stride=BLK), :]

    def send(src, dst, ssem, rsem, k):
        return pltpu.make_async_remote_copy(
            src_ref=src, dst_ref=dst, send_sem=ssem, recv_sem=rsem,
            device_id=place_of(k), device_id_type=MESH,
        )

    def wait_for(ref, sem):
        pltpu.make_async_copy(ref, ref, sem).wait()

    def send_d(k):
        send(dsrc, rd.at[pl.ds(g, 1)], sd, qd, k).start()

    def send_w(k):
        send(wbuf.at[k], warr.at[me], sw, qw, k).start()

    def send_f(h, k):
        send(fbuf.at[h, k], farr.at[h, me], sf.at[h], qf.at[h], k).start()

    def to_low(act):
        @pl.loop(1, low)
        def _(s):
            act(lax.rem(me + s, low))

    def to_high(zz, act):
        @pl.loop(0, plane)
        def _(s):
            act(plane * zz + lax.rem(me + s, plane))

    pl.semaphore_wait(barrier, low - 1)

    @pl.loop(0, plane * z)
    def _(k):
        pl.semaphore_signal(above.at[z], inc=1, device_id=place_of(k), device_id_type=MESH)

    @pl.loop(1, 2 * (z + 1))
    def _(s):
        send_d(lax.rem(g + s, 2 * (z + 1)) * owners + p)

    own = [pltpu.make_async_copy(wbuf.at[me], warr.at[me], local.at[0])]
    own += [pltpu.make_async_copy(fbuf.at[h, me], farr.at[h, me], local.at[1 + h]) for h in range(2)]
    to_low(send_w)
    own[0].start()

    xpad[:, :LANES] = jnp.zeros((NB * BLK, LANES), jnp.float32)
    xpad[:, columns:] = jnp.zeros((NB * BLK, LANES), jnp.float32)
    loads[0].wait()
    xpad[:, SIDE:SIDE + columns] = img[...]
    xh, xl = halves(xpad[...])
    for n in (4, 5, 6):
        loads[n].wait()
    which = psf[p]
    rows = NB * BLK
    ah, al = halves(
        jnp.concatenate([rows_t[b * rows:(b + 1) * rows, :] * coef[b, which] for b in range(BASES)], axis=0)
    )
    yh, yl = halves(dot(ah, xh) + dot(al, xh) + dot(ah, xl))
    wide = LANES + 2 * SIDE
    loads[7].wait()
    double = jnp.zeros((tiles * rows, 2 * LANES), jnp.float32)
    one = jnp.zeros((tiles * rows, LANES), jnp.float32)
    for b in range(BASES):
        def windows(y):
            return jnp.concatenate(
                [y[b * rows:(b + 1) * rows, t * LANES:t * LANES + wide] for t in range(tiles)], axis=0
            )
        double = double + dot(windows(yh), cols_t[b * wide:(b + 1) * wide, :])
        one = one + dot(windows(yl), cols_t[b * wide:(b + 1) * wide, :LANES])
    smooth = double[:, :LANES] + double[:, LANES:] + one
    for t in range(tiles):
        for h in range(2):
            for i in range(owners):
                k, at = t * owners + i, t * rows + (h * owners + i) * 8
                fbuf[h, k] = wbuf[k, h] * smooth[at:at + 8]

    to_low(functools.partial(send_f, 0))
    own[1].start()

    @pl.loop(z + 1, chips)
    def _(zz):
        pl.semaphore_wait(above.at[zz], plane)

        @pl.loop(0, 2)
        def _(c):
            send_d((2 * zz + c) * owners + p)

        to_high(zz, send_w)
        to_high(zz, functools.partial(send_f, 0))

    to_low(functools.partial(send_f, 1))
    own[2].start()

    @pl.loop(z + 1, chips)
    def _(zz):
        to_high(zz, functools.partial(send_f, 1))

    wait_for(rd.at[pl.ds(0, groups - 1)], qd)

    many = devices * 8
    k_lane = lax.broadcasted_iota(jnp.int32, (1, many), 1)
    goal = jnp.zeros((1, many), jnp.int32)
    run = 8 * owners
    for h in range(groups):
        turned = pltpu.roll(rd[h], (h * run) % LANES, 1)
        goal = jnp.where(k_lane // run == h, jnp.concatenate([turned] * (many // LANES), axis=1), goal)
    slots = owners * NS
    goal = goal + slots * lax.rem(k_lane // NB, 2)
    row = lax.broadcasted_iota(jnp.int32, (2 * slots, many), 0)
    hot = jnp.where(row == goal, 1.0, 0.0).astype(jnp.bfloat16)

    wait_for(warr.at[pl.ds(0, devices - 1)], qw)
    own[0].wait()
    high, low_part = halves(jnp.concatenate([warr[:, h].reshape(many, LANES) for h in range(2)], axis=1))
    scale = 1.0 / jnp.maximum(dot(hot, high) + dot(hot, low_part), 1.0)

    def piece(h, there, q):
        k = (2 * there + core) * owners + q
        return send(cbuf.at[h, q], out.at[h, g, p], so.at[h], qo.at[h, z], k)

    own_o = [pltpu.make_async_copy(cbuf.at[h, p], out.at[h, g, p], local.at[3 + h]) for h in range(2)]

    def add_up(h):
        wait_for(farr.at[h, pl.ds(0, devices - 1)], qf.at[h])
        own[1 + h].wait()
        high, low_part = halves(farr[h].reshape(many, LANES))
        ratio = (dot(hot, high) + dot(hot, low_part)) * scale[:, h * LANES:(h + 1) * LANES]
        for q in range(owners):
            for r2 in range(2):
                cbuf[h, q, r2] = ratio[r2 * slots + q * NS:r2 * slots + (q + 1) * NS]

        @pl.loop(1, chips)
        def _(s):
            @pl.loop(0, owners)
            def _(v):
                piece(h, lax.rem(z + s, chips), lax.rem(p + v, owners)).start()

        @pl.loop(1, owners)
        def _(v):
            piece(h, z, lax.rem(p + v, owners)).start()

        own_o[h].start()

    sibling = (z * 2 + 1 - core) * owners + p

    def across(h, there, side):
        j = there * 2 + side
        return send(out.at[h, j], out.at[h, j], sx.at[h, there], qx.at[h, there], sibling)

    def relay(h):
        for s in range(chips):
            there = lax.rem(z + s, chips)
            if s == 0:
                wait_for(out.at[h, g, pl.ds(0, owners - 1)], qo.at[h, z])
                own_o[h].wait()
            else:
                wait_for(out.at[h, there * 2 + core], qo.at[h, there])
            across(h, there, core).start()

    add_up(0)
    add_up(1)
    relay(0)
    relay(1)
    for h in range(2):
        for s in range(chips):
            across(h, lax.rem(z + s, chips), 1 - core).wait_recv()

    wait_for(rd.at[pl.ds(0, groups - 1)], sd)
    wait_for(warr.at[pl.ds(0, devices - 1)], sw)
    for h in range(2):
        wait_for(farr.at[h, pl.ds(0, devices - 1)], sf.at[h])
        for s in range(1, chips):
            wait_for(out.at[h, 0], so.at[h])
        wait_for(out.at[h, 0, pl.ds(0, owners - 1)], so.at[h])
        for there in range(chips):
            across(h, there, core).wait_send()


def lay_out(parts, out, flat, sem):
    copies = []
    for t in range(flat.shape[0]):
        at = slice(t * LANES, (t + 1) * LANES)
        for h in range(2):
            for i in range(BLK // 4):
                for r2 in range(2):
                    flat[t, pl.ds(h * 8 + i * 2 + r2, NS, stride=BLK), :] = parts[h, t, i, r2]
        copy = pltpu.make_async_copy(flat.at[t], out.at[:, at], sem.at[t])
        copy.start()
        copies.append(copy)
    for copy in copies:
        copy.wait()


def on_device_kernel(image, variance, block_count, slot_start, psf_index, coef_table):
    groups, owners = lax.axis_size("expgrp"), lax.axis_size("patch")
    devices = groups * owners
    rows, columns = image.shape
    slots = owners * NS
    dma = pltpu.SemaphoreType.DMA
    f32 = jnp.float32
    hbm = pl.BlockSpec(memory_space=pltpu.HBM)
    parts = pl.pallas_call(
        functools.partial(kernel, groups, owners),
        out_shape=pltpu.VMEM((2, groups, owners, 2, NS, LANES), f32),
        in_specs=[hbm] * 8,
        out_specs=pl.BlockSpec(memory_space=pl.ANY),
        scratch_shapes=[
            pltpu.VMEM((rows, columns), f32),
            pltpu.VMEM((rows, columns), f32),
            pltpu.SMEM(block_count.shape, jnp.int32),
            pltpu.SMEM(slot_start.shape, jnp.int32),
            pltpu.SMEM(psf_index.shape, jnp.int32),
            pltpu.SMEM(coef_table.shape[::-1], f32),
            pltpu.VMEM((BASES * rows, rows), f32),
            pltpu.VMEM((BASES * (LANES + 2 * SIDE), 2 * LANES), jnp.bfloat16),
            pltpu.VMEM((rows, columns + 2 * SIDE), f32),
            pltpu.VMEM((columns // LANES, rows, LANES), f32),
            pltpu.VMEM((devices, 2, 8, LANES), f32),
            pltpu.VMEM((2, devices, 8, LANES), f32),
            pltpu.VMEM((1, 1, LANES), jnp.int32),
            pltpu.VMEM((devices, 2, 8, LANES), f32),
            pltpu.VMEM((2, devices, 8, LANES), f32),
            pltpu.VMEM((groups, 1, LANES), jnp.int32),
            pltpu.VMEM((2, owners, 2, NS, LANES), f32),
            dma, dma, dma((2,)), dma((2,)), dma, dma,
            dma((2,)), dma((2, groups // 2)),
            dma((2, groups // 2)), dma((2, groups // 2)),
            pltpu.SemaphoreType.REGULAR((groups // 2,)),
            dma((5,)), dma((8,)),
        ],
        compiler_params=pltpu.CompilerParams(
            collective_id=0, has_side_effects=True, vmem_limit_bytes=56 * 1024 * 1024
        ),
    )(
        image, variance, block_count, slot_start, psf_index, coef_table.T,
        jnp.asarray(np_row_table()), jnp.asarray(np_column_table()),
    )
    return pl.pallas_call(
        lay_out,
        out_shape=jax.ShapeDtypeStruct((NS * BLK, columns), f32),
        in_specs=[pl.BlockSpec(memory_space=pltpu.VMEM)],
        out_specs=hbm,
        scratch_shapes=[pltpu.VMEM((columns // LANES, NS * BLK, LANES), f32), dma((columns // LANES,))],
        compiler_params=pltpu.CompilerParams(vmem_limit_bytes=16 * 1024 * 1024),
    )(parts)


def profile(offsets, deviation):
    offset_range = jnp.arange(-KH, KH + 1).astype(jnp.float32)
    total = jnp.sum(jnp.exp(-offset_range * offset_range / (2.0 * deviation * deviation)))
    spacing = offsets.astype(jnp.float32)
    return jnp.where(
        jnp.abs(offsets) <= KH,
        jnp.exp(-spacing * spacing / (2.0 * deviation * deviation)) / total,
        jnp.float32(0.0),
    )


def column_table(tile_width):
    inner_index = jnp.arange(3 * tile_width, dtype=jnp.int32)[:, None]
    outer_index = jnp.arange(tile_width, dtype=jnp.int32)[None, :]
    columns_list = [
        profile(inner_index - tile_width - outer_index, deviation) for deviation in SIGMAS
    ]
    return jnp.concatenate(columns_list, axis=1)


def row_table(height):
    row_index = jnp.arange(height, dtype=jnp.int32)
    return jnp.stack(
        [profile(row_index[None, :] - row_index[:, None], deviation) for deviation in SIGMAS]
    )


def matched(blocks, mixing):
    number, height, columns = blocks.shape
    tile_width = 128
    tile_count = columns // tile_width
    parted = blocks.reshape(number, height, tile_count, tile_width)
    blank = jnp.zeros((number, height, 1, tile_width), jnp.float32)
    behind = jnp.concatenate([blank, parted[:, :, :-1]], axis=2)
    follow = jnp.concatenate([parted[:, :, 1:], blank], axis=2)
    joined = jnp.concatenate([behind, parted, follow], axis=3)
    across = jnp.einsum("nrti,ik->nrtk", joined, column_table(tile_width), precision=highest)
    across = across.reshape(number, height, tile_count, len(SIGMAS), tile_width)
    vertical = mixing[:, :, None, None] * row_table(height)[None]
    result = jnp.einsum("nbrk,nktbc->nrtc", vertical, across, precision=highest)
    return result.reshape(number, height, columns)


def on_device(image, variance, block_count, slot_start, psf_index, coef_table):
    owners = lax.axis_size("patch")
    own_index = lax.axis_index("patch")
    tile_rows, columns = image.shape
    number = tile_rows // BLK
    lookup = (
        jnp.arange(coef_table.shape[0], dtype=jnp.int32)[None, :] == psf_index[:, None]
    ).astype(jnp.float32)
    mixing = jnp.sum(lookup[:, :, None] * coef_table[None, :, :], axis=1)
    own_count = lax.dynamic_index_in_dim(block_count, own_index, 0, keepdims=False)
    before = jnp.arange(owners)[None, :] < jnp.arange(owners)[:, None]
    firsts = jnp.sum(jnp.where(before, own_count[None, :], 0), axis=1)
    places = jnp.arange(CAP, dtype=jnp.int32)
    source = firsts[:, None] + places[None, :]
    filled = places[None, :] < own_count[:, None]

    def arrange(values):
        total = jnp.zeros((owners, CAP, BLK, columns), jnp.float32)
        for n in range(number):
            here = (source == n) & filled
            total = jnp.where(here[:, :, None, None], values[n][None, None], total)
        return total

    image_blocks = image.reshape(number, BLK, columns)
    scale_blocks = variance.reshape(number, BLK, columns)
    raw_blocks = lax.all_to_all(
        arrange(image_blocks), "patch", split_axis=0, concat_axis=0, tiled=True
    )
    raw_scales = lax.all_to_all(
        arrange(scale_blocks), "patch", split_axis=0, concat_axis=0, tiled=True
    )
    senders = raw_blocks.shape[0]
    slot_count = raw_blocks.shape[1]
    present = raw_scales > 0.0
    weights = jnp.where(present, 1.0 / jnp.where(present, raw_scales, 1.0), 0.0)
    spread = jnp.broadcast_to(mixing[:, None, :], (senders, slot_count, mixing.shape[1]))
    smooth = matched(
        raw_blocks.reshape(senders * slot_count, BLK, columns),
        spread.reshape(senders * slot_count, mixing.shape[1]),
    )
    arrived_flux = weights * smooth.reshape(raw_blocks.shape)
    arrived_count = lax.dynamic_index_in_dim(block_count, own_index, 1, keepdims=False)
    arrived_start = lax.dynamic_index_in_dim(slot_start, own_index, 1, keepdims=False)
    slots = jnp.arange(NS, dtype=jnp.int32)
    target = (places[None, :] < arrived_count[:, None])[None] & (
        arrived_start[:, None] + places[None, :] == slots[:, None, None]
    )
    layout = target.astype(jnp.float32)
    flux_sum = jnp.einsum("spj,pjrw->srw", layout, arrived_flux, precision=highest).reshape(
        NS * BLK, columns
    )
    weight_sum = jnp.einsum("spj,pjrw->srw", layout, weights, precision=highest).reshape(
        NS * BLK, columns
    )
    flux_total, weight_total = lax.psum((flux_sum, weight_sum), "expgrp")
    return flux_total / jnp.maximum(weight_total, 1.0)


def route(groups, owners, image, *rest):
    rows, columns = image.shape
    fits = rows == NB * BLK and columns == LANES * groups and BLK == 4 * owners and groups % 2 == 0
    return on_device_kernel(image, *rest) if fits else on_device(image, *rest)


def solution(mesh):
    in_specs = (
        P(("expgrp", "patch"), None),
        P(("expgrp", "patch"), None),
        P("expgrp", None),
        P("expgrp", None),
        P("expgrp"),
        P(),
    )
    out_specs = P("patch", None)
    return jax.shard_map(
        functools.partial(route, mesh.shape["expgrp"], mesh.shape["patch"]),
        mesh=mesh, in_specs=in_specs, out_specs=out_specs, check_vma=False,
    )
```

```python
import functools
import math

import jax
import jax.numpy as jnp
import numpy as np
from jax import lax
from jax.experimental import pallas as pl
from jax.experimental.pallas import tpu as pltpu
from jax.sharding import PartitionSpec as P

BLK = 16
CAP = 2
NS = 16
KH = 10
NB = 4
LANES = 128
SIDE = 64
SENDS = ((((2,), (1,)), ((2,), (0,)), ((1,), (3,)), ((1,), (2,))), (((1,), (2,), (3,)), ((2,), (3,), (0,)), ((3,), (0,), (1,)), ((0,), (1,), (2,))))
TAKES = ((((1, None), (2, None), (3, None)), ((2, 0), (0, None), (3, 0)), ((3, None), (1, 3), (0, 3)), ((2, None), (1, None), (0, None))), (((1, None), (2, None), (3, None)), ((2, None), (0, None), (3, None)), ((3, None), (1, None), (0, None)), ((2, None), (1, None), (0, None))))
PASSES = (((), ((2, 0), (3, 0)), ((1, 3), (0, 3)), ()), ((), (), (), ()))


SIGMAS = (0.75, 1.5, 3.0)
BASES = len(SIGMAS)
highest = lax.Precision.HIGHEST
MESH = pl.DeviceIdType.MESH


def np_profile(offsets, deviation):
    every = np.arange(-KH, KH + 1, dtype=np.float64)
    total = np.sum(np.exp(-every * every / (2.0 * deviation * deviation)))
    spacing = offsets.astype(np.float64)
    return np.where(
        np.abs(offsets) <= KH, np.exp(-spacing * spacing / (2.0 * deviation * deviation)) / total, 0.0
    ).astype(np.float32)


def np_row_table():
    row = np.arange(BLK * NB)
    r, n = row // NB, row % NB
    m, k = row // BLK, row % BLK
    same = (n[:, None] == m[None, :]).astype(np.float32)
    return np.concatenate([same * np_profile(k[None, :] - r[:, None], s) for s in SIGMAS], axis=0)


def np_column_table():
    i = np.arange(LANES + 2 * SIDE)[:, None]
    c = np.arange(LANES)[None, :]
    whole = np.concatenate([np_profile(i - SIDE - c, s) for s in SIGMAS], axis=0)
    high = whole.astype(jnp.bfloat16)
    low = (whole - high.astype(np.float32)).astype(jnp.bfloat16)
    return np.concatenate([high, low], axis=1)


def halves(x):
    high = x.astype(jnp.bfloat16)
    return high, (x - high.astype(jnp.float32)).astype(jnp.bfloat16)


def dot(a, b):
    return jnp.dot(a, b, preferred_element_type=jnp.float32)


def kernel(groups, owners, *refs):
    inputs, out, stage = refs[:8], refs[8], refs[9:17]
    (xpad, vbuf, wbuf, fbuf, dsrc, warr, farr, rd, cbuf,
     sw, qw, sf, qf, sd, qd, so, qo, sr, sx, qx, above, local, fetch) = refs[17:]
    loads = [pltpu.make_async_copy(a, b, fetch.at[n]) for n, (a, b) in enumerate(zip(inputs, stage))]
    for n in (1, 2, 3, 0, 4, 5, 6, 7):
        loads[n].start()
    img, var, count, start, psf, coef, rows_t, cols_t = stage
    g, p = lax.axis_index("expgrp"), lax.axis_index("patch")
    devices = groups * owners
    me = g * owners + p
    columns = img.shape[1]
    tiles = columns // LANES
    chips = groups // 2
    plane = 2 * owners
    z, core = g // 2, g % 2
    last = devices - plane
    late = z == chips - 1
    known = jnp.where(late, devices, last)

    def place_of(k):
        return (k // owners, lax.rem(k, owners))

    barrier = pltpu.get_barrier_semaphore()

    @pl.loop(1, jnp.where(late, plane, devices))
    def _(s):
        k = jnp.where(late, last + lax.rem(me - last + s, plane), lax.rem(me + s, devices))
        pl.semaphore_signal(barrier, inc=1, device_id=place_of(k), device_id_type=MESH)

    loads[2].wait()
    loads[3].wait()
    lane = lax.broadcasted_iota(jnp.int32, (1, LANES), 1)
    place = jnp.zeros((1, LANES), jnp.int32)
    block = lax.rem(lane, NB)
    for e in range(owners):
        first = jnp.int32(0)
        for q in range(owners):
            n_here = count[e, q]
            base = q * NS + start[e, q] - first
            inside = (lane // 8 == e) & (block >= first) & (block < first + n_here)
            place = jnp.where(inside, base + block, place)
            first = first + n_here
    dsrc[0] = place
    rd[g] = place
    loads[1].wait()

    for t in range(tiles):
        vbuf[t] = 1.0 / var[:, t * LANES:(t + 1) * LANES]
        for r in range(BLK):
            h, i = r // 8, (r // 2) % 4
            wbuf[t * owners + i, h, (r % 2) * NB:(r % 2) * NB + NB, :] = vbuf[t, pl.ds(r, NB, stride=BLK), :]

    def send(src, dst, ssem, rsem, k):
        return pltpu.make_async_remote_copy(
            src_ref=src, dst_ref=dst, send_sem=ssem, recv_sem=rsem,
            device_id=place_of(k), device_id_type=MESH,
        )

    def wait_for(ref, sem):
        pltpu.make_async_copy(ref, ref, sem).wait()

    def send_d(k):
        send(dsrc, rd.at[pl.ds(g, 1)], sd, qd, k).start()

    def send_w(k):
        send(wbuf.at[k], warr.at[me], sw, qw, k).start()

    def send_f(h, k):
        send(fbuf.at[h, k], farr.at[h, me], sf.at[h], qf.at[h], k).start()

    def to_all(act):
        @pl.loop(1, devices)
        def _(s):
            act(lax.rem(me + s, devices))

    pl.semaphore_wait(barrier, known - 1)

    @pl.when(late)
    def _():
        @pl.loop(0, last)
        def _(k):
            pl.semaphore_signal(above, inc=1, device_id=place_of(k), device_id_type=MESH)

    @pl.loop(1, known // owners)
    def _(s):
        send_d(lax.rem(g + s, known // owners) * owners + p)

    own = [pltpu.make_async_copy(wbuf.at[me], warr.at[me], local.at[0])]
    own += [pltpu.make_async_copy(fbuf.at[h, me], farr.at[h, me], local.at[1 + h]) for h in range(2)]
    @pl.loop(1, known)
    def _(s):
        send_w(lax.rem(me + s, known))

    own[0].start()

    xpad[:, :LANES] = jnp.zeros((NB * BLK, LANES), jnp.float32)
    xpad[:, columns:] = jnp.zeros((NB * BLK, LANES), jnp.float32)
    loads[0].wait()
    xpad[:, SIDE:SIDE + columns] = img[...]
    xh, xl = halves(xpad[...])
    for n in (4, 5, 6):
        loads[n].wait()
    which = psf[p]
    rows = NB * BLK
    ah, al = halves(
        jnp.concatenate([rows_t[b * rows:(b + 1) * rows, :] * coef[b, which] for b in range(BASES)], axis=0)
    )
    yh, yl = halves(dot(ah, xh) + dot(al, xh) + dot(ah, xl))
    wide = LANES + 2 * SIDE
    loads[7].wait()
    double = jnp.zeros((tiles * rows, 2 * LANES), jnp.float32)
    one = jnp.zeros((tiles * rows, LANES), jnp.float32)
    for b in range(BASES):
        def windows(y):
            return jnp.concatenate(
                [y[b * rows:(b + 1) * rows, t * LANES:t * LANES + wide] for t in range(tiles)], axis=0
            )
        double = double + dot(windows(yh), cols_t[b * wide:(b + 1) * wide, :])
        one = one + dot(windows(yl), cols_t[b * wide:(b + 1) * wide, :LANES])
    smooth = double[:, :LANES] + double[:, LANES:] + one
    for t in range(tiles):
        for h in range(2):
            for i in range(owners):
                k, at = t * owners + i, t * rows + (h * owners + i) * 8
                fbuf[h, k] = wbuf[k, h] * smooth[at:at + 8]

    @pl.when(z < chips - 1)
    def _():
        pl.semaphore_wait(above, plane)

        @pl.loop(0, 2)
        def _(c):
            send_d((groups - 2 + c) * owners + p)

        @pl.loop(0, plane)
        def _(s):
            send_w(last + lax.rem(me + s, plane))

    for h in range(2):
        to_all(functools.partial(send_f, h))
        own[1 + h].start()

    wait_for(rd.at[pl.ds(0, groups - 1)], qd)

    many = devices * 8
    k_lane = lax.broadcasted_iota(jnp.int32, (1, many), 1)
    goal = jnp.zeros((1, many), jnp.int32)
    run = 8 * owners
    for h in range(groups):
        turned = pltpu.roll(rd[h], (h * run) % LANES, 1)
        goal = jnp.where(k_lane // run == h, jnp.concatenate([turned] * (many // LANES), axis=1), goal)
    slots = owners * NS
    goal = goal + slots * lax.rem(k_lane // NB, 2)
    row = lax.broadcasted_iota(jnp.int32, (2 * slots, many), 0)
    hot = jnp.where(row == goal, 1.0, 0.0).astype(jnp.bfloat16)

    wait_for(warr.at[pl.ds(0, devices - 1)], qw)
    own[0].wait()
    high, low_part = halves(jnp.concatenate([warr[:, h].reshape(many, LANES) for h in range(2)], axis=1))
    scale = 1.0 / jnp.maximum(dot(hot, high) + dot(hot, low_part), 1.0)

    def piece(h, there, q):
        k = (2 * there + core) * owners + q
        return send(cbuf.at[h, q], out.at[h, g, p], so.at[h], qo.at[h, z], k)

    own_o = [pltpu.make_async_copy(cbuf.at[h, p], out.at[h, g, p], local.at[3 + h]) for h in range(2)]

    def on_plane(table, act):
        for zz, entries in enumerate(table):
            if entries:
                @pl.when(z == zz)
                def _(entries=entries):
                    for entry in entries:
                        act(*entry)

    def each_piece(h, act):
        def to_plane(there):
            for v in range(owners):
                act(piece(h, there, lax.rem(p + v, owners)))

        on_plane(SENDS[h], to_plane)
        for v in range(1, owners):
            act(piece(h, z, lax.rem(p + v, owners)))

    def add_up(h):
        wait_for(farr.at[h, pl.ds(0, devices - 1)], qf.at[h])
        own[1 + h].wait()
        high, low_part = halves(farr[h].reshape(many, LANES))
        ratio = (dot(hot, high) + dot(hot, low_part)) * scale[:, h * LANES:(h + 1) * LANES]
        for q in range(owners):
            for r2 in range(2):
                cbuf[h, q, r2] = ratio[r2 * slots + q * NS:r2 * slots + (q + 1) * NS]
        each_piece(h, lambda copy: copy.start())
        own_o[h].start()

    sibling = (z * 2 + 1 - core) * owners + p

    def across(h, there, side):
        j = there * 2 + side
        return send(out.at[h, j], out.at[h, j], sx.at[h, there], qx.at[h, there], sibling)

    def onward(h, there, to):
        j = there * 2 + core
        return send(out.at[h, j], out.at[h, j], sr.at[h, there], qo.at[h, there], (to * 2 + core) * owners + p)

    def take(h, there, to):
        wait_for(out.at[h, there * 2 + core], qo.at[h, there])
        if to is not None:
            onward(h, there, to).start()
        across(h, there, core).start()

    def relay(h):
        wait_for(out.at[h, g, pl.ds(0, owners - 1)], qo.at[h, z])
        own_o[h].wait()
        across(h, z, core).start()
        on_plane(TAKES[h], functools.partial(take, h))

    add_up(0)
    add_up(1)
    relay(0)
    relay(1)
    for h in range(2):
        for there in range(chips):
            across(h, there, 1 - core).wait_recv()

    wait_for(rd.at[pl.ds(0, groups - 1)], sd)
    wait_for(warr.at[pl.ds(0, devices - 1)], sw)
    for h in range(2):
        wait_for(farr.at[h, pl.ds(0, devices - 1)], sf.at[h])
        each_piece(h, lambda copy: copy.wait_send())
        on_plane(PASSES[h], lambda there, to: onward(h, there, to).wait_send())
        for there in range(chips):
            across(h, there, core).wait_send()


def lay_out(parts, out, flat, sem):
    copies = []
    for t in range(flat.shape[0]):
        at = slice(t * LANES, (t + 1) * LANES)
        for h in range(2):
            for i in range(BLK // 4):
                for r2 in range(2):
                    flat[t, pl.ds(h * 8 + i * 2 + r2, NS, stride=BLK), :] = parts[h, t, i, r2]
        copy = pltpu.make_async_copy(flat.at[t], out.at[:, at], sem.at[t])
        copy.start()
        copies.append(copy)
    for copy in copies:
        copy.wait()


def on_device_kernel(image, variance, block_count, slot_start, psf_index, coef_table):
    groups, owners = lax.axis_size("expgrp"), lax.axis_size("patch")
    devices = groups * owners
    rows, columns = image.shape
    slots = owners * NS
    dma = pltpu.SemaphoreType.DMA
    f32 = jnp.float32
    hbm = pl.BlockSpec(memory_space=pltpu.HBM)
    parts = pl.pallas_call(
        functools.partial(kernel, groups, owners),
        out_shape=pltpu.VMEM((2, groups, owners, 2, NS, LANES), f32),
        in_specs=[hbm] * 8,
        out_specs=pl.BlockSpec(memory_space=pl.ANY),
        scratch_shapes=[
            pltpu.VMEM((rows, columns), f32),
            pltpu.VMEM((rows, columns), f32),
            pltpu.SMEM(block_count.shape, jnp.int32),
            pltpu.SMEM(slot_start.shape, jnp.int32),
            pltpu.SMEM(psf_index.shape, jnp.int32),
            pltpu.SMEM(coef_table.shape[::-1], f32),
            pltpu.VMEM((BASES * rows, rows), f32),
            pltpu.VMEM((BASES * (LANES + 2 * SIDE), 2 * LANES), jnp.bfloat16),
            pltpu.VMEM((rows, columns + 2 * SIDE), f32),
            pltpu.VMEM((columns // LANES, rows, LANES), f32),
            pltpu.VMEM((devices, 2, 8, LANES), f32),
            pltpu.VMEM((2, devices, 8, LANES), f32),
            pltpu.VMEM((1, 1, LANES), jnp.int32),
            pltpu.VMEM((devices, 2, 8, LANES), f32),
            pltpu.VMEM((2, devices, 8, LANES), f32),
            pltpu.VMEM((groups, 1, LANES), jnp.int32),
            pltpu.VMEM((2, owners, 2, NS, LANES), f32),
            dma, dma, dma((2,)), dma((2,)), dma, dma,
            dma((2,)), dma((2, groups // 2)), dma((2, groups // 2)),
            dma((2, groups // 2)), dma((2, groups // 2)),
            pltpu.SemaphoreType.REGULAR,
            dma((5,)), dma((8,)),
        ],
        compiler_params=pltpu.CompilerParams(
            collective_id=0, has_side_effects=True, vmem_limit_bytes=56 * 1024 * 1024
        ),
    )(
        image, variance, block_count, slot_start, psf_index, coef_table.T,
        jnp.asarray(np_row_table()), jnp.asarray(np_column_table()),
    )
    return pl.pallas_call(
        lay_out,
        out_shape=jax.ShapeDtypeStruct((NS * BLK, columns), f32),
        in_specs=[pl.BlockSpec(memory_space=pltpu.VMEM)],
        out_specs=hbm,
        scratch_shapes=[pltpu.VMEM((columns // LANES, NS * BLK, LANES), f32), dma((columns // LANES,))],
        compiler_params=pltpu.CompilerParams(vmem_limit_bytes=16 * 1024 * 1024),
    )(parts)


def profile(offsets, deviation):
    offset_range = jnp.arange(-KH, KH + 1).astype(jnp.float32)
    total = jnp.sum(jnp.exp(-offset_range * offset_range / (2.0 * deviation * deviation)))
    spacing = offsets.astype(jnp.float32)
    return jnp.where(
        jnp.abs(offsets) <= KH,
        jnp.exp(-spacing * spacing / (2.0 * deviation * deviation)) / total,
        jnp.float32(0.0),
    )


def column_table(tile_width):
    inner_index = jnp.arange(3 * tile_width, dtype=jnp.int32)[:, None]
    outer_index = jnp.arange(tile_width, dtype=jnp.int32)[None, :]
    columns_list = [
        profile(inner_index - tile_width - outer_index, deviation) for deviation in SIGMAS
    ]
    return jnp.concatenate(columns_list, axis=1)


def row_table(height):
    row_index = jnp.arange(height, dtype=jnp.int32)
    return jnp.stack(
        [profile(row_index[None, :] - row_index[:, None], deviation) for deviation in SIGMAS]
    )


def matched(blocks, mixing):
    number, height, columns = blocks.shape
    tile_width = 128
    tile_count = columns // tile_width
    parted = blocks.reshape(number, height, tile_count, tile_width)
    blank = jnp.zeros((number, height, 1, tile_width), jnp.float32)
    behind = jnp.concatenate([blank, parted[:, :, :-1]], axis=2)
    follow = jnp.concatenate([parted[:, :, 1:], blank], axis=2)
    joined = jnp.concatenate([behind, parted, follow], axis=3)
    across = jnp.einsum("nrti,ik->nrtk", joined, column_table(tile_width), precision=highest)
    across = across.reshape(number, height, tile_count, len(SIGMAS), tile_width)
    vertical = mixing[:, :, None, None] * row_table(height)[None]
    result = jnp.einsum("nbrk,nktbc->nrtc", vertical, across, precision=highest)
    return result.reshape(number, height, columns)


def on_device(image, variance, block_count, slot_start, psf_index, coef_table):
    owners = lax.axis_size("patch")
    own_index = lax.axis_index("patch")
    tile_rows, columns = image.shape
    number = tile_rows // BLK
    lookup = (
        jnp.arange(coef_table.shape[0], dtype=jnp.int32)[None, :] == psf_index[:, None]
    ).astype(jnp.float32)
    mixing = jnp.sum(lookup[:, :, None] * coef_table[None, :, :], axis=1)
    own_count = lax.dynamic_index_in_dim(block_count, own_index, 0, keepdims=False)
    before = jnp.arange(owners)[None, :] < jnp.arange(owners)[:, None]
    firsts = jnp.sum(jnp.where(before, own_count[None, :], 0), axis=1)
    places = jnp.arange(CAP, dtype=jnp.int32)
    source = firsts[:, None] + places[None, :]
    filled = places[None, :] < own_count[:, None]

    def arrange(values):
        total = jnp.zeros((owners, CAP, BLK, columns), jnp.float32)
        for n in range(number):
            here = (source == n) & filled
            total = jnp.where(here[:, :, None, None], values[n][None, None], total)
        return total

    image_blocks = image.reshape(number, BLK, columns)
    scale_blocks = variance.reshape(number, BLK, columns)
    raw_blocks = lax.all_to_all(
        arrange(image_blocks), "patch", split_axis=0, concat_axis=0, tiled=True
    )
    raw_scales = lax.all_to_all(
        arrange(scale_blocks), "patch", split_axis=0, concat_axis=0, tiled=True
    )
    senders = raw_blocks.shape[0]
    slot_count = raw_blocks.shape[1]
    present = raw_scales > 0.0
    weights = jnp.where(present, 1.0 / jnp.where(present, raw_scales, 1.0), 0.0)
    spread = jnp.broadcast_to(mixing[:, None, :], (senders, slot_count, mixing.shape[1]))
    smooth = matched(
        raw_blocks.reshape(senders * slot_count, BLK, columns),
        spread.reshape(senders * slot_count, mixing.shape[1]),
    )
    arrived_flux = weights * smooth.reshape(raw_blocks.shape)
    arrived_count = lax.dynamic_index_in_dim(block_count, own_index, 1, keepdims=False)
    arrived_start = lax.dynamic_index_in_dim(slot_start, own_index, 1, keepdims=False)
    slots = jnp.arange(NS, dtype=jnp.int32)
    target = (places[None, :] < arrived_count[:, None])[None] & (
        arrived_start[:, None] + places[None, :] == slots[:, None, None]
    )
    layout = target.astype(jnp.float32)
    flux_sum = jnp.einsum("spj,pjrw->srw", layout, arrived_flux, precision=highest).reshape(
        NS * BLK, columns
    )
    weight_sum = jnp.einsum("spj,pjrw->srw", layout, weights, precision=highest).reshape(
        NS * BLK, columns
    )
    flux_total, weight_total = lax.psum((flux_sum, weight_sum), "expgrp")
    return flux_total / jnp.maximum(weight_total, 1.0)


def route(groups, owners, image, *rest):
    rows, columns = image.shape
    fits = rows == NB * BLK and columns == LANES * groups and BLK == 4 * owners and groups % 2 == 0
    return on_device_kernel(image, *rest) if fits else on_device(image, *rest)


def solution(mesh):
    in_specs = (
        P(("expgrp", "patch"), None),
        P(("expgrp", "patch"), None),
        P("expgrp", None),
        P("expgrp", None),
        P("expgrp"),
        P(),
    )
    out_specs = P("patch", None)
    return jax.shard_map(
        functools.partial(route, mesh.shape["expgrp"], mesh.shape["patch"]),
        mesh=mesh, in_specs=in_specs, out_specs=out_specs, check_vma=False,
    )
```

```python
import functools
import math

import jax
import jax.numpy as jnp
import numpy as np
from jax import lax
from jax.experimental import pallas as pl
from jax.experimental.pallas import tpu as pltpu
from jax.sharding import PartitionSpec as P

BLK = 16
CAP = 2
NS = 16
KH = 10
NB = 4
LANES = 128
SIDE = 64
EARLY = (((2, 0), (1, 0), (0, 1)), ((2, 0), (0, 0), (1, 1)), ((0, 0), (1, 0), (2, 1)), ((0, 0), (1, 0), (2, 0), (3, 1)))
ORDER = (((2, 0), (3, 0), (1, 0), (0, 1)), ((2, 0), (3, 0), (1, 1), (0, 0)), ((1, 0), (0, 0), (3, 0), (2, 1)), ((1, 0), (0, 0), (2, 0), (3, 1)))
SENDS = ((((2,), (1,)), ((2,), (0,)), ((1,), (3,)), ((1,), (2,))), (((1,), (2,), (3,)), ((2,), (3,), (0,)), ((3,), (0,), (1,)), ((0,), (1,), (2,))))
TAKES = ((((1, None), (2, None), (3, None)), ((2, 0), (0, None), (3, 0)), ((3, None), (1, 3), (0, 3)), ((2, None), (1, None), (0, None))), (((1, None), (2, None), (3, None)), ((2, None), (0, None), (3, None)), ((3, None), (1, None), (0, None)), ((2, None), (1, None), (0, None))))
PASSES = (((), ((2, 0), (3, 0)), ((1, 3), (0, 3)), ()), ((), (), (), ()))


SIGMAS = (0.75, 1.5, 3.0)
BASES = len(SIGMAS)
highest = lax.Precision.HIGHEST
MESH = pl.DeviceIdType.MESH


def np_profile(offsets, deviation):
    every = np.arange(-KH, KH + 1, dtype=np.float64)
    total = np.sum(np.exp(-every * every / (2.0 * deviation * deviation)))
    spacing = offsets.astype(np.float64)
    return np.where(
        np.abs(offsets) <= KH, np.exp(-spacing * spacing / (2.0 * deviation * deviation)) / total, 0.0
    ).astype(np.float32)


def np_row_table():
    row = np.arange(BLK * NB)
    r, n = row // NB, row % NB
    m, k = row // BLK, row % BLK
    same = (n[:, None] == m[None, :]).astype(np.float32)
    return np.concatenate([same * np_profile(k[None, :] - r[:, None], s) for s in SIGMAS], axis=0)


def np_column_table():
    i = np.arange(LANES + 2 * SIDE)[:, None]
    c = np.arange(LANES)[None, :]
    whole = np.concatenate([np_profile(i - SIDE - c, s) for s in SIGMAS], axis=0)
    high = whole.astype(jnp.bfloat16)
    low = (whole - high.astype(np.float32)).astype(jnp.bfloat16)
    return np.concatenate([high, low], axis=1)


def halves(x):
    high = x.astype(jnp.bfloat16)
    return high, (x - high.astype(jnp.float32)).astype(jnp.bfloat16)


def dot(a, b):
    return jnp.dot(a, b, preferred_element_type=jnp.float32)


def kernel(groups, owners, *refs):
    inputs, out, stage = refs[:8], refs[8], refs[9:17]
    (xpad, vbuf, both, dsrc, arrived, rd, cbuf,
     sb, qb, sd, qd, so, qo, sr, sx, qx, above, local, fetch) = refs[17:]
    loads = [pltpu.make_async_copy(a, b, fetch.at[n]) for n, (a, b) in enumerate(zip(inputs, stage))]
    for n in (1, 2, 3, 0, 4, 5, 6, 7):
        loads[n].start()
    img, var, count, start, psf, coef, rows_t, cols_t = stage
    g, p = lax.axis_index("expgrp"), lax.axis_index("patch")
    devices = groups * owners
    me = g * owners + p
    columns = img.shape[1]
    tiles = columns // LANES
    chips = groups // 2
    plane = 2 * owners
    z, core = g // 2, g % 2
    last = devices - plane
    late = z == chips - 1
    known = jnp.where(late, devices, last)

    def place_of(k):
        return (k // owners, lax.rem(k, owners))

    barrier = pltpu.get_barrier_semaphore()

    @pl.loop(1, jnp.where(late, plane, devices))
    def _(s):
        k = jnp.where(late, last + lax.rem(me - last + s, plane), lax.rem(me + s, devices))
        pl.semaphore_signal(barrier, inc=1, device_id=place_of(k), device_id_type=MESH)

    loads[2].wait()
    loads[3].wait()
    lane = lax.broadcasted_iota(jnp.int32, (1, LANES), 1)
    place = jnp.zeros((1, LANES), jnp.int32)
    block = lax.rem(lane, NB)
    for e in range(owners):
        first = jnp.int32(0)
        for q in range(owners):
            n_here = count[e, q]
            base = q * NS + start[e, q] - first
            inside = (lane // 8 == e) & (block >= first) & (block < first + n_here)
            place = jnp.where(inside, base + block, place)
            first = first + n_here
    dsrc[0] = place
    rd[g] = place
    loads[1].wait()

    for t in range(tiles):
        vbuf[t] = 1.0 / var[:, t * LANES:(t + 1) * LANES]
        for r in range(BLK):
            h, i = r // 8, (r // 2) % 4
            both[h, t * owners + i, 1, (r % 2) * NB:(r % 2) * NB + NB, :] = vbuf[t, pl.ds(r, NB, stride=BLK), :]

    def send(src, dst, ssem, rsem, k):
        return pltpu.make_async_remote_copy(
            src_ref=src, dst_ref=dst, send_sem=ssem, recv_sem=rsem,
            device_id=place_of(k), device_id_type=MESH,
        )

    def wait_for(ref, sem):
        pltpu.make_async_copy(ref, ref, sem).wait()

    def send_d(k):
        send(dsrc, rd.at[pl.ds(g, 1)], sd, qd, k).start()

    def send_b(h, k):
        send(both.at[h, k], arrived.at[h, me], sb.at[h], qb.at[h], k).start()

    def on_plane(table, act):
        for zz, entries in enumerate(table):
            if entries:
                @pl.when(z == zz)
                def _(entries=entries):
                    for entry in entries:
                        act(*entry)

    def to_planes(table, act):
        def to_plane(there, first):
            @pl.loop(first, plane)
            def _(s):
                act(plane * there + lax.rem(me + s, plane))

        on_plane(table, to_plane)

    xpad[:, :LANES] = jnp.zeros((NB * BLK, LANES), jnp.float32)
    xpad[:, columns:] = jnp.zeros((NB * BLK, LANES), jnp.float32)
    loads[0].wait()
    xpad[:, SIDE:SIDE + columns] = img[...]
    xh, xl = halves(xpad[...])
    for n in (4, 5, 6):
        loads[n].wait()
    which = psf[p]
    loads[7].wait()
    rows, part = NB * BLK, NB * BLK // 2
    wide = LANES + 2 * SIDE

    def smooth(h):
        ah, al = halves(jnp.concatenate(
            [rows_t[b * rows + h * part:b * rows + (h + 1) * part, :] * coef[b, which] for b in range(BASES)], axis=0
        ))
        yh, yl = halves(dot(ah, xh) + dot(al, xh) + dot(ah, xl))
        double = jnp.zeros((tiles * part, 2 * LANES), jnp.float32)
        one = jnp.zeros((tiles * part, LANES), jnp.float32)
        for b in range(BASES):
            def windows(y):
                return jnp.concatenate(
                    [y[b * part:(b + 1) * part, t * LANES:t * LANES + wide] for t in range(tiles)], axis=0
                )
            double = double + dot(windows(yh), cols_t[b * wide:(b + 1) * wide, :])
            one = one + dot(windows(yl), cols_t[b * wide:(b + 1) * wide, :LANES])
        total = double[:, :LANES] + double[:, LANES:] + one
        for t in range(tiles):
            for i in range(owners):
                k, at = t * owners + i, t * part + i * 8
                both[h, k, 0] = both[h, k, 1] * total[at:at + 8]

    smooth(0)
    pl.semaphore_wait(barrier, known - 1)

    @pl.when(late)
    def _():
        @pl.loop(0, last)
        def _(k):
            pl.semaphore_signal(above, inc=1, device_id=place_of(k), device_id_type=MESH)

    @pl.loop(1, known // owners)
    def _(s):
        send_d(lax.rem(g + s, known // owners) * owners + p)

    own = [pltpu.make_async_copy(both.at[h, me], arrived.at[h, me], local.at[h]) for h in range(2)]
    to_planes(EARLY, functools.partial(send_b, 0))
    own[0].start()
    smooth(1)

    @pl.when(z < chips - 1)
    def _():
        pl.semaphore_wait(above, plane)

        @pl.loop(0, 2)
        def _(c):
            send_d((groups - 2 + c) * owners + p)

        @pl.loop(0, plane)
        def _(s):
            send_b(0, last + lax.rem(me + s, plane))

    to_planes(ORDER, functools.partial(send_b, 1))
    own[1].start()

    wait_for(rd.at[pl.ds(0, groups - 1)], qd)

    many = devices * 8
    k_lane = lax.broadcasted_iota(jnp.int32, (1, many), 1)
    goal = jnp.zeros((1, many), jnp.int32)
    run = 8 * owners
    for h in range(groups):
        turned = pltpu.roll(rd[h], (h * run) % LANES, 1)
        goal = jnp.where(k_lane // run == h, jnp.concatenate([turned] * (many // LANES), axis=1), goal)
    slots = owners * NS
    goal = goal + slots * lax.rem(k_lane // NB, 2)
    row = lax.broadcasted_iota(jnp.int32, (2 * slots, many), 0)
    hot = jnp.where(row == goal, 1.0, 0.0).astype(jnp.bfloat16)

    def piece(h, there, q):
        k = (2 * there + core) * owners + q
        return send(cbuf.at[h, q], out.at[h, g, p], so.at[h], qo.at[h, z], k)

    own_o = [pltpu.make_async_copy(cbuf.at[h, p], out.at[h, g, p], local.at[2 + h]) for h in range(2)]

    def each_piece(h, act):
        def to_plane(there):
            for v in range(owners):
                act(piece(h, there, lax.rem(p + v, owners)))

        on_plane(SENDS[h], to_plane)
        for v in range(1, owners):
            act(piece(h, z, lax.rem(p + v, owners)))

    def add_up(h):
        wait_for(arrived.at[h, pl.ds(0, devices - 1)], qb.at[h])
        own[h].wait()
        high, low_part = halves(jnp.concatenate([arrived[h, :, n].reshape(many, LANES) for n in range(2)], axis=1))
        total = dot(hot, high) + dot(hot, low_part)
        ratio = total[:, :LANES] / jnp.maximum(total[:, LANES:], 1.0)
        for q in range(owners):
            for r2 in range(2):
                cbuf[h, q, r2] = ratio[r2 * slots + q * NS:r2 * slots + (q + 1) * NS]
        each_piece(h, lambda copy: copy.start())
        own_o[h].start()

    sibling = (z * 2 + 1 - core) * owners + p

    def across(h, there, side):
        j = there * 2 + side
        return send(out.at[h, j], out.at[h, j], sx.at[h, there], qx.at[h, there], sibling)

    def onward(h, there, to):
        j = there * 2 + core
        return send(out.at[h, j], out.at[h, j], sr.at[h, there], qo.at[h, there], (to * 2 + core) * owners + p)

    def take(h, there, to):
        wait_for(out.at[h, there * 2 + core], qo.at[h, there])
        if to is not None:
            onward(h, there, to).start()
        across(h, there, core).start()

    def relay(h):
        wait_for(out.at[h, g, pl.ds(0, owners - 1)], qo.at[h, z])
        own_o[h].wait()
        across(h, z, core).start()
        on_plane(TAKES[h], functools.partial(take, h))

    add_up(0)
    add_up(1)
    relay(0)
    relay(1)
    for h in range(2):
        for there in range(chips):
            across(h, there, 1 - core).wait_recv()

    wait_for(rd.at[pl.ds(0, groups - 1)], sd)
    for h in range(2):
        wait_for(arrived.at[h, pl.ds(0, devices - 1)], sb.at[h])
        each_piece(h, lambda copy: copy.wait_send())
        on_plane(PASSES[h], lambda there, to: onward(h, there, to).wait_send())
        for there in range(chips):
            across(h, there, core).wait_send()


def lay_out(parts, out, flat, sem):
    copies = []
    for t in range(flat.shape[0]):
        at = slice(t * LANES, (t + 1) * LANES)
        for h in range(2):
            for i in range(BLK // 4):
                for r2 in range(2):
                    flat[t, pl.ds(h * 8 + i * 2 + r2, NS, stride=BLK), :] = parts[h, t, i, r2]
        copy = pltpu.make_async_copy(flat.at[t], out.at[:, at], sem.at[t])
        copy.start()
        copies.append(copy)
    for copy in copies:
        copy.wait()


def on_device_kernel(image, variance, block_count, slot_start, psf_index, coef_table):
    groups, owners = lax.axis_size("expgrp"), lax.axis_size("patch")
    devices = groups * owners
    rows, columns = image.shape
    slots = owners * NS
    dma = pltpu.SemaphoreType.DMA
    f32 = jnp.float32
    hbm = pl.BlockSpec(memory_space=pltpu.HBM)
    parts = pl.pallas_call(
        functools.partial(kernel, groups, owners),
        out_shape=pltpu.VMEM((2, groups, owners, 2, NS, LANES), f32),
        in_specs=[hbm] * 8,
        out_specs=pl.BlockSpec(memory_space=pl.ANY),
        scratch_shapes=[
            pltpu.VMEM((rows, columns), f32),
            pltpu.VMEM((rows, columns), f32),
            pltpu.SMEM(block_count.shape, jnp.int32),
            pltpu.SMEM(slot_start.shape, jnp.int32),
            pltpu.SMEM(psf_index.shape, jnp.int32),
            pltpu.SMEM(coef_table.shape[::-1], f32),
            pltpu.VMEM((BASES * rows, rows), f32),
            pltpu.VMEM((BASES * (LANES + 2 * SIDE), 2 * LANES), jnp.bfloat16),
            pltpu.VMEM((rows, columns + 2 * SIDE), f32),
            pltpu.VMEM((columns // LANES, rows, LANES), f32),
            pltpu.VMEM((2, devices, 2, 8, LANES), f32),
            pltpu.VMEM((1, 1, LANES), jnp.int32),
            pltpu.VMEM((2, devices, 2, 8, LANES), f32),
            pltpu.VMEM((groups, 1, LANES), jnp.int32),
            pltpu.VMEM((2, owners, 2, NS, LANES), f32),
            dma((2,)), dma((2,)), dma, dma,
            dma((2,)), dma((2, groups // 2)), dma((2, groups // 2)),
            dma((2, groups // 2)), dma((2, groups // 2)),
            pltpu.SemaphoreType.REGULAR,
            dma((4,)), dma((8,)),
        ],
        compiler_params=pltpu.CompilerParams(
            collective_id=0, has_side_effects=True, vmem_limit_bytes=56 * 1024 * 1024
        ),
    )(
        image, variance, block_count, slot_start, psf_index, coef_table.T,
        jnp.asarray(np_row_table()), jnp.asarray(np_column_table()),
    )
    return pl.pallas_call(
        lay_out,
        out_shape=jax.ShapeDtypeStruct((NS * BLK, columns), f32),
        in_specs=[pl.BlockSpec(memory_space=pltpu.VMEM)],
        out_specs=hbm,
        scratch_shapes=[pltpu.VMEM((columns // LANES, NS * BLK, LANES), f32), dma((columns // LANES,))],
        compiler_params=pltpu.CompilerParams(vmem_limit_bytes=16 * 1024 * 1024),
    )(parts)


def profile(offsets, deviation):
    offset_range = jnp.arange(-KH, KH + 1).astype(jnp.float32)
    total = jnp.sum(jnp.exp(-offset_range * offset_range / (2.0 * deviation * deviation)))
    spacing = offsets.astype(jnp.float32)
    return jnp.where(
        jnp.abs(offsets) <= KH,
        jnp.exp(-spacing * spacing / (2.0 * deviation * deviation)) / total,
        jnp.float32(0.0),
    )


def column_table(tile_width):
    inner_index = jnp.arange(3 * tile_width, dtype=jnp.int32)[:, None]
    outer_index = jnp.arange(tile_width, dtype=jnp.int32)[None, :]
    columns_list = [
        profile(inner_index - tile_width - outer_index, deviation) for deviation in SIGMAS
    ]
    return jnp.concatenate(columns_list, axis=1)


def row_table(height):
    row_index = jnp.arange(height, dtype=jnp.int32)
    return jnp.stack(
        [profile(row_index[None, :] - row_index[:, None], deviation) for deviation in SIGMAS]
    )


def matched(blocks, mixing):
    number, height, columns = blocks.shape
    tile_width = 128
    tile_count = columns // tile_width
    parted = blocks.reshape(number, height, tile_count, tile_width)
    blank = jnp.zeros((number, height, 1, tile_width), jnp.float32)
    behind = jnp.concatenate([blank, parted[:, :, :-1]], axis=2)
    follow = jnp.concatenate([parted[:, :, 1:], blank], axis=2)
    joined = jnp.concatenate([behind, parted, follow], axis=3)
    across = jnp.einsum("nrti,ik->nrtk", joined, column_table(tile_width), precision=highest)
    across = across.reshape(number, height, tile_count, len(SIGMAS), tile_width)
    vertical = mixing[:, :, None, None] * row_table(height)[None]
    result = jnp.einsum("nbrk,nktbc->nrtc", vertical, across, precision=highest)
    return result.reshape(number, height, columns)


def on_device(image, variance, block_count, slot_start, psf_index, coef_table):
    owners = lax.axis_size("patch")
    own_index = lax.axis_index("patch")
    tile_rows, columns = image.shape
    number = tile_rows // BLK
    lookup = (
        jnp.arange(coef_table.shape[0], dtype=jnp.int32)[None, :] == psf_index[:, None]
    ).astype(jnp.float32)
    mixing = jnp.sum(lookup[:, :, None] * coef_table[None, :, :], axis=1)
    own_count = lax.dynamic_index_in_dim(block_count, own_index, 0, keepdims=False)
    before = jnp.arange(owners)[None, :] < jnp.arange(owners)[:, None]
    firsts = jnp.sum(jnp.where(before, own_count[None, :], 0), axis=1)
    places = jnp.arange(CAP, dtype=jnp.int32)
    source = firsts[:, None] + places[None, :]
    filled = places[None, :] < own_count[:, None]

    def arrange(values):
        total = jnp.zeros((owners, CAP, BLK, columns), jnp.float32)
        for n in range(number):
            here = (source == n) & filled
            total = jnp.where(here[:, :, None, None], values[n][None, None], total)
        return total

    image_blocks = image.reshape(number, BLK, columns)
    scale_blocks = variance.reshape(number, BLK, columns)
    raw_blocks = lax.all_to_all(
        arrange(image_blocks), "patch", split_axis=0, concat_axis=0, tiled=True
    )
    raw_scales = lax.all_to_all(
        arrange(scale_blocks), "patch", split_axis=0, concat_axis=0, tiled=True
    )
    senders = raw_blocks.shape[0]
    slot_count = raw_blocks.shape[1]
    present = raw_scales > 0.0
    weights = jnp.where(present, 1.0 / jnp.where(present, raw_scales, 1.0), 0.0)
    spread = jnp.broadcast_to(mixing[:, None, :], (senders, slot_count, mixing.shape[1]))
    smooth = matched(
        raw_blocks.reshape(senders * slot_count, BLK, columns),
        spread.reshape(senders * slot_count, mixing.shape[1]),
    )
    arrived_flux = weights * smooth.reshape(raw_blocks.shape)
    arrived_count = lax.dynamic_index_in_dim(block_count, own_index, 1, keepdims=False)
    arrived_start = lax.dynamic_index_in_dim(slot_start, own_index, 1, keepdims=False)
    slots = jnp.arange(NS, dtype=jnp.int32)
    target = (places[None, :] < arrived_count[:, None])[None] & (
        arrived_start[:, None] + places[None, :] == slots[:, None, None]
    )
    layout = target.astype(jnp.float32)
    flux_sum = jnp.einsum("spj,pjrw->srw", layout, arrived_flux, precision=highest).reshape(
        NS * BLK, columns
    )
    weight_sum = jnp.einsum("spj,pjrw->srw", layout, weights, precision=highest).reshape(
        NS * BLK, columns
    )
    flux_total, weight_total = lax.psum((flux_sum, weight_sum), "expgrp")
    return flux_total / jnp.maximum(weight_total, 1.0)


def route(groups, owners, image, *rest):
    rows, columns = image.shape
    fits = rows == NB * BLK and columns == LANES * groups and BLK == 4 * owners and groups % 2 == 0
    return on_device_kernel(image, *rest) if fits else on_device(image, *rest)


def solution(mesh):
    in_specs = (
        P(("expgrp", "patch"), None),
        P(("expgrp", "patch"), None),
        P("expgrp", None),
        P("expgrp", None),
        P("expgrp"),
        P(),
    )
    out_specs = P("patch", None)
    return jax.shard_map(
        functools.partial(route, mesh.shape["expgrp"], mesh.shape["patch"]),
        mesh=mesh, in_specs=in_specs, out_specs=out_specs, check_vma=False,
    )
```

```python
import functools
import math

import jax
import jax.numpy as jnp
import numpy as np
from jax import lax
from jax.experimental import pallas as pl
from jax.experimental.pallas import tpu as pltpu
from jax.sharding import PartitionSpec as P

BLK = 16
CAP = 2
NS = 16
KH = 10
NB = 4
LANES = 128
SIDE = 64
EARLY = (((2, 0), (1, 0), (0, 1)), ((2, 0), (0, 0), (1, 1)), ((0, 0), (1, 0), (2, 1)), ((0, 0), (1, 0), (2, 0), (3, 1)))
ORDER = (((2, 0), (3, 0), (0, 1), (1, 0)), ((2, 0), (3, 0), (1, 1), (0, 0)), ((1, 0), (0, 0), (2, 1), (3, 0)), ((1, 0), (0, 0), (3, 1), (2, 0)))
SENDS = ((((2,), (1,)), ((2,), (3,), (0,)), ((1,), (0,), (3,)), ((1,), (2,))), (((1,), (2,), (3,)), ((2,), (3,), (0,)), ((3,), (0,), (1,)), ((0,), (1,), (2,))))
TAKES = ((((1, None), (2, None), (3, None)), ((2, None), (0, None), (3, 0)), ((3, None), (1, None), (0, 3)), ((2, None), (1, None), (0, None))), (((1, None), (2, None), (3, None)), ((2, None), (0, None), (3, None)), ((3, None), (1, None), (0, None)), ((2, None), (1, None), (0, None))))
PASSES = (((), ((3, 0),), ((0, 3),), ()), ((), (), (), ()))


SIGMAS = (0.75, 1.5, 3.0)
BASES = len(SIGMAS)
highest = lax.Precision.HIGHEST
MESH = pl.DeviceIdType.MESH


def np_profile(offsets, deviation):
    every = np.arange(-KH, KH + 1, dtype=np.float64)
    total = np.sum(np.exp(-every * every / (2.0 * deviation * deviation)))
    spacing = offsets.astype(np.float64)
    return np.where(
        np.abs(offsets) <= KH, np.exp(-spacing * spacing / (2.0 * deviation * deviation)) / total, 0.0
    ).astype(np.float32)


def np_row_table():
    row = np.arange(BLK * NB)
    r, n = row // NB, row % NB
    m, k = row // BLK, row % BLK
    same = (n[:, None] == m[None, :]).astype(np.float32)
    return np.concatenate([same * np_profile(k[None, :] - r[:, None], s) for s in SIGMAS], axis=0)


def np_column_table():
    i = np.arange(LANES + 2 * SIDE)[:, None]
    c = np.arange(LANES)[None, :]
    whole = np.concatenate([np_profile(i - SIDE - c, s) for s in SIGMAS], axis=0)
    high = whole.astype(jnp.bfloat16)
    low = (whole - high.astype(np.float32)).astype(jnp.bfloat16)
    return np.concatenate([high, low], axis=1)


def halves(x):
    high = x.astype(jnp.bfloat16)
    return high, (x - high.astype(jnp.float32)).astype(jnp.bfloat16)


def dot(a, b):
    return jnp.dot(a, b, preferred_element_type=jnp.float32)


def kernel(groups, owners, *refs):
    inputs, out, stage = refs[:8], refs[8], refs[9:17]
    (xpad, vbuf, both, dsrc, arrived, rd, cbuf,
     sb, qb, sd, qd, so, qo, sr, sx, qx, above, local, fetch) = refs[17:]
    loads = [pltpu.make_async_copy(a, b, fetch.at[n]) for n, (a, b) in enumerate(zip(inputs, stage))]
    for n in (1, 2, 3, 0, 4, 5, 6, 7):
        loads[n].start()
    img, var, count, start, psf, coef, rows_t, cols_t = stage
    g, p = lax.axis_index("expgrp"), lax.axis_index("patch")
    devices = groups * owners
    me = g * owners + p
    columns = img.shape[1]
    tiles = columns // LANES
    chips = groups // 2
    plane = 2 * owners
    z, core = g // 2, g % 2
    last = devices - plane
    late = z == chips - 1
    known = jnp.where(late, devices, last)

    def place_of(k):
        return (k // owners, lax.rem(k, owners))

    barrier = pltpu.get_barrier_semaphore()

    @pl.loop(1, jnp.where(late, plane, devices))
    def _(s):
        k = jnp.where(late, last + lax.rem(me - last + s, plane), lax.rem(me + s, devices))
        pl.semaphore_signal(barrier, inc=1, device_id=place_of(k), device_id_type=MESH)

    loads[2].wait()
    loads[3].wait()
    lane = lax.broadcasted_iota(jnp.int32, (1, LANES), 1)
    place = jnp.zeros((1, LANES), jnp.int32)
    block = lax.rem(lane, NB)
    for e in range(owners):
        first = jnp.int32(0)
        for q in range(owners):
            n_here = count[e, q]
            base = q * NS + start[e, q] - first
            inside = (lane // 8 == e) & (block >= first) & (block < first + n_here)
            place = jnp.where(inside, base + block, place)
            first = first + n_here
    dsrc[0] = place
    rd[g] = place
    loads[1].wait()

    for t in range(tiles):
        vbuf[t] = 1.0 / var[:, t * LANES:(t + 1) * LANES]
        for r in range(BLK):
            h, i = r // 8, (r // 2) % 4
            both[h, t * owners + i, 1, (r % 2) * NB:(r % 2) * NB + NB, :] = vbuf[t, pl.ds(r, NB, stride=BLK), :]

    def send(src, dst, ssem, rsem, k):
        return pltpu.make_async_remote_copy(
            src_ref=src, dst_ref=dst, send_sem=ssem, recv_sem=rsem,
            device_id=place_of(k), device_id_type=MESH,
        )

    def wait_for(ref, sem):
        pltpu.make_async_copy(ref, ref, sem).wait()

    def send_d(k):
        send(dsrc, rd.at[pl.ds(g, 1)], sd, qd, k).start()

    def send_b(h, k):
        send(both.at[h, k], arrived.at[h, me], sb.at[h], qb.at[h], k).start()

    def on_plane(table, act):
        for zz, entries in enumerate(table):
            if entries:
                @pl.when(z == zz)
                def _(entries=entries):
                    for entry in entries:
                        act(*entry)

    def to_planes(table, act):
        def to_plane(there, first):
            @pl.loop(first, plane)
            def _(s):
                act(plane * there + lax.rem(me + s, plane))

        on_plane(table, to_plane)

    xpad[:, :LANES] = jnp.zeros((NB * BLK, LANES), jnp.float32)
    xpad[:, columns:] = jnp.zeros((NB * BLK, LANES), jnp.float32)
    loads[0].wait()
    xpad[:, SIDE:SIDE + columns] = img[...]
    xh, xl = halves(xpad[...])
    for n in (4, 5, 6):
        loads[n].wait()
    which = psf[p]
    loads[7].wait()
    rows, part = NB * BLK, NB * BLK // 2
    wide = LANES + 2 * SIDE

    def smooth(h):
        ah, al = halves(jnp.concatenate(
            [rows_t[b * rows + h * part:b * rows + (h + 1) * part, :] * coef[b, which] for b in range(BASES)], axis=0
        ))
        yh, yl = halves(dot(ah, xh) + dot(al, xh) + dot(ah, xl))
        double = jnp.zeros((tiles * part, 2 * LANES), jnp.float32)
        one = jnp.zeros((tiles * part, LANES), jnp.float32)
        for b in range(BASES):
            def windows(y):
                return jnp.concatenate(
                    [y[b * part:(b + 1) * part, t * LANES:t * LANES + wide] for t in range(tiles)], axis=0
                )
            double = double + dot(windows(yh), cols_t[b * wide:(b + 1) * wide, :])
            one = one + dot(windows(yl), cols_t[b * wide:(b + 1) * wide, :LANES])
        total = double[:, :LANES] + double[:, LANES:] + one
        for t in range(tiles):
            for i in range(owners):
                k, at = t * owners + i, t * part + i * 8
                both[h, k, 0] = both[h, k, 1] * total[at:at + 8]

    smooth(0)
    pl.semaphore_wait(barrier, known - 1)

    @pl.when(late)
    def _():
        @pl.loop(0, last)
        def _(k):
            pl.semaphore_signal(above, inc=1, device_id=place_of(k), device_id_type=MESH)

    @pl.loop(1, known // owners)
    def _(s):
        send_d(lax.rem(g + s, known // owners) * owners + p)

    own = [pltpu.make_async_copy(both.at[h, me], arrived.at[h, me], local.at[h]) for h in range(2)]
    to_planes(EARLY, functools.partial(send_b, 0))
    own[0].start()
    smooth(1)

    @pl.when(z < chips - 1)
    def _():
        pl.semaphore_wait(above, plane)

        @pl.loop(0, 2)
        def _(c):
            send_d((groups - 2 + c) * owners + p)

        @pl.loop(0, plane)
        def _(s):
            send_b(0, last + lax.rem(me + s, plane))

    to_planes(ORDER, functools.partial(send_b, 1))
    own[1].start()

    wait_for(rd.at[pl.ds(0, groups - 1)], qd)

    many = devices * 8
    k_lane = lax.broadcasted_iota(jnp.int32, (1, many), 1)
    goal = jnp.zeros((1, many), jnp.int32)
    run = 8 * owners
    for h in range(groups):
        turned = pltpu.roll(rd[h], (h * run) % LANES, 1)
        goal = jnp.where(k_lane // run == h, jnp.concatenate([turned] * (many // LANES), axis=1), goal)
    slots = owners * NS
    goal = goal + slots * lax.rem(k_lane // NB, 2)
    row = lax.broadcasted_iota(jnp.int32, (2 * slots, many), 0)
    hot = jnp.where(row == goal, 1.0, 0.0).astype(jnp.bfloat16)

    def piece(h, there, q):
        k = (2 * there + core) * owners + q
        return send(cbuf.at[h, q], out.at[h, g, p], so.at[h], qo.at[h, z], k)

    own_o = [pltpu.make_async_copy(cbuf.at[h, p], out.at[h, g, p], local.at[2 + h]) for h in range(2)]

    def each_piece(h, act):
        def to_plane(there):
            for v in range(owners):
                act(piece(h, there, lax.rem(p + v, owners)))

        on_plane(SENDS[h], to_plane)
        for v in range(1, owners):
            act(piece(h, z, lax.rem(p + v, owners)))

    def add_up(h):
        wait_for(arrived.at[h, pl.ds(0, devices - 1)], qb.at[h])
        own[h].wait()
        high, low_part = halves(jnp.concatenate([arrived[h, :, n].reshape(many, LANES) for n in range(2)], axis=1))
        total = dot(hot, high) + dot(hot, low_part)
        ratio = total[:, :LANES] / jnp.maximum(total[:, LANES:], 1.0)
        for q in range(owners):
            for r2 in range(2):
                cbuf[h, q, r2] = ratio[r2 * slots + q * NS:r2 * slots + (q + 1) * NS]
        each_piece(h, lambda copy: copy.start())
        own_o[h].start()

    sibling = (z * 2 + 1 - core) * owners + p

    def across(h, there, side):
        j = there * 2 + side
        return send(out.at[h, j], out.at[h, j], sx.at[h, there], qx.at[h, there], sibling)

    def onward(h, there, to):
        j = there * 2 + core
        return send(out.at[h, j], out.at[h, j], sr.at[h, there], qo.at[h, there], (to * 2 + core) * owners + p)

    def take(h, there, to):
        wait_for(out.at[h, there * 2 + core], qo.at[h, there])
        if to is not None:
            onward(h, there, to).start()
        across(h, there, core).start()

    def relay(h):
        wait_for(out.at[h, g, pl.ds(0, owners - 1)], qo.at[h, z])
        own_o[h].wait()
        across(h, z, core).start()
        on_plane(TAKES[h], functools.partial(take, h))

    add_up(0)
    add_up(1)
    relay(0)
    relay(1)
    for h in range(2):
        for there in range(chips):
            across(h, there, 1 - core).wait_recv()

    wait_for(rd.at[pl.ds(0, groups - 1)], sd)
    for h in range(2):
        wait_for(arrived.at[h, pl.ds(0, devices - 1)], sb.at[h])
        each_piece(h, lambda copy: copy.wait_send())
        on_plane(PASSES[h], lambda there, to: onward(h, there, to).wait_send())
        for there in range(chips):
            across(h, there, core).wait_send()


def lay_out(parts, out, flat, sem):
    copies = []
    for t in range(flat.shape[0]):
        at = slice(t * LANES, (t + 1) * LANES)
        for h in range(2):
            for i in range(BLK // 4):
                for r2 in range(2):
                    flat[t, pl.ds(h * 8 + i * 2 + r2, NS, stride=BLK), :] = parts[h, t, i, r2]
        copy = pltpu.make_async_copy(flat.at[t], out.at[:, at], sem.at[t])
        copy.start()
        copies.append(copy)
    for copy in copies:
        copy.wait()


def on_device_kernel(image, variance, block_count, slot_start, psf_index, coef_table):
    groups, owners = lax.axis_size("expgrp"), lax.axis_size("patch")
    devices = groups * owners
    rows, columns = image.shape
    slots = owners * NS
    dma = pltpu.SemaphoreType.DMA
    f32 = jnp.float32
    hbm = pl.BlockSpec(memory_space=pltpu.HBM)
    parts = pl.pallas_call(
        functools.partial(kernel, groups, owners),
        out_shape=pltpu.VMEM((2, groups, owners, 2, NS, LANES), f32),
        in_specs=[hbm] * 8,
        out_specs=pl.BlockSpec(memory_space=pl.ANY),
        scratch_shapes=[
            pltpu.VMEM((rows, columns), f32),
            pltpu.VMEM((rows, columns), f32),
            pltpu.SMEM(block_count.shape, jnp.int32),
            pltpu.SMEM(slot_start.shape, jnp.int32),
            pltpu.SMEM(psf_index.shape, jnp.int32),
            pltpu.SMEM(coef_table.shape[::-1], f32),
            pltpu.VMEM((BASES * rows, rows), f32),
            pltpu.VMEM((BASES * (LANES + 2 * SIDE), 2 * LANES), jnp.bfloat16),
            pltpu.VMEM((rows, columns + 2 * SIDE), f32),
            pltpu.VMEM((columns // LANES, rows, LANES), f32),
            pltpu.VMEM((2, devices, 2, 8, LANES), f32),
            pltpu.VMEM((1, 1, LANES), jnp.int32),
            pltpu.VMEM((2, devices, 2, 8, LANES), f32),
            pltpu.VMEM((groups, 1, LANES), jnp.int32),
            pltpu.VMEM((2, owners, 2, NS, LANES), f32),
            dma((2,)), dma((2,)), dma, dma,
            dma((2,)), dma((2, groups // 2)), dma((2, groups // 2)),
            dma((2, groups // 2)), dma((2, groups // 2)),
            pltpu.SemaphoreType.REGULAR,
            dma((4,)), dma((8,)),
        ],
        compiler_params=pltpu.CompilerParams(
            collective_id=0, has_side_effects=True, vmem_limit_bytes=56 * 1024 * 1024
        ),
    )(
        image, variance, block_count, slot_start, psf_index, coef_table.T,
        jnp.asarray(np_row_table()), jnp.asarray(np_column_table()),
    )
    return pl.pallas_call(
        lay_out,
        out_shape=jax.ShapeDtypeStruct((NS * BLK, columns), f32),
        in_specs=[pl.BlockSpec(memory_space=pltpu.VMEM)],
        out_specs=hbm,
        scratch_shapes=[pltpu.VMEM((columns // LANES, NS * BLK, LANES), f32), dma((columns // LANES,))],
        compiler_params=pltpu.CompilerParams(vmem_limit_bytes=16 * 1024 * 1024),
    )(parts)


def profile(offsets, deviation):
    offset_range = jnp.arange(-KH, KH + 1).astype(jnp.float32)
    total = jnp.sum(jnp.exp(-offset_range * offset_range / (2.0 * deviation * deviation)))
    spacing = offsets.astype(jnp.float32)
    return jnp.where(
        jnp.abs(offsets) <= KH,
        jnp.exp(-spacing * spacing / (2.0 * deviation * deviation)) / total,
        jnp.float32(0.0),
    )


def column_table(tile_width):
    inner_index = jnp.arange(3 * tile_width, dtype=jnp.int32)[:, None]
    outer_index = jnp.arange(tile_width, dtype=jnp.int32)[None, :]
    columns_list = [
        profile(inner_index - tile_width - outer_index, deviation) for deviation in SIGMAS
    ]
    return jnp.concatenate(columns_list, axis=1)


def row_table(height):
    row_index = jnp.arange(height, dtype=jnp.int32)
    return jnp.stack(
        [profile(row_index[None, :] - row_index[:, None], deviation) for deviation in SIGMAS]
    )


def matched(blocks, mixing):
    number, height, columns = blocks.shape
    tile_width = 128
    tile_count = columns // tile_width
    parted = blocks.reshape(number, height, tile_count, tile_width)
    blank = jnp.zeros((number, height, 1, tile_width), jnp.float32)
    behind = jnp.concatenate([blank, parted[:, :, :-1]], axis=2)
    follow = jnp.concatenate([parted[:, :, 1:], blank], axis=2)
    joined = jnp.concatenate([behind, parted, follow], axis=3)
    across = jnp.einsum("nrti,ik->nrtk", joined, column_table(tile_width), precision=highest)
    across = across.reshape(number, height, tile_count, len(SIGMAS), tile_width)
    vertical = mixing[:, :, None, None] * row_table(height)[None]
    result = jnp.einsum("nbrk,nktbc->nrtc", vertical, across, precision=highest)
    return result.reshape(number, height, columns)


def on_device(image, variance, block_count, slot_start, psf_index, coef_table):
    owners = lax.axis_size("patch")
    own_index = lax.axis_index("patch")
    tile_rows, columns = image.shape
    number = tile_rows // BLK
    lookup = (
        jnp.arange(coef_table.shape[0], dtype=jnp.int32)[None, :] == psf_index[:, None]
    ).astype(jnp.float32)
    mixing = jnp.sum(lookup[:, :, None] * coef_table[None, :, :], axis=1)
    own_count = lax.dynamic_index_in_dim(block_count, own_index, 0, keepdims=False)
    before = jnp.arange(owners)[None, :] < jnp.arange(owners)[:, None]
    firsts = jnp.sum(jnp.where(before, own_count[None, :], 0), axis=1)
    places = jnp.arange(CAP, dtype=jnp.int32)
    source = firsts[:, None] + places[None, :]
    filled = places[None, :] < own_count[:, None]

    def arrange(values):
        total = jnp.zeros((owners, CAP, BLK, columns), jnp.float32)
        for n in range(number):
            here = (source == n) & filled
            total = jnp.where(here[:, :, None, None], values[n][None, None], total)
        return total

    image_blocks = image.reshape(number, BLK, columns)
    scale_blocks = variance.reshape(number, BLK, columns)
    raw_blocks = lax.all_to_all(
        arrange(image_blocks), "patch", split_axis=0, concat_axis=0, tiled=True
    )
    raw_scales = lax.all_to_all(
        arrange(scale_blocks), "patch", split_axis=0, concat_axis=0, tiled=True
    )
    senders = raw_blocks.shape[0]
    slot_count = raw_blocks.shape[1]
    present = raw_scales > 0.0
    weights = jnp.where(present, 1.0 / jnp.where(present, raw_scales, 1.0), 0.0)
    spread = jnp.broadcast_to(mixing[:, None, :], (senders, slot_count, mixing.shape[1]))
    smooth = matched(
        raw_blocks.reshape(senders * slot_count, BLK, columns),
        spread.reshape(senders * slot_count, mixing.shape[1]),
    )
    arrived_flux = weights * smooth.reshape(raw_blocks.shape)
    arrived_count = lax.dynamic_index_in_dim(block_count, own_index, 1, keepdims=False)
    arrived_start = lax.dynamic_index_in_dim(slot_start, own_index, 1, keepdims=False)
    slots = jnp.arange(NS, dtype=jnp.int32)
    target = (places[None, :] < arrived_count[:, None])[None] & (
        arrived_start[:, None] + places[None, :] == slots[:, None, None]
    )
    layout = target.astype(jnp.float32)
    flux_sum = jnp.einsum("spj,pjrw->srw", layout, arrived_flux, precision=highest).reshape(
        NS * BLK, columns
    )
    weight_sum = jnp.einsum("spj,pjrw->srw", layout, weights, precision=highest).reshape(
        NS * BLK, columns
    )
    flux_total, weight_total = lax.psum((flux_sum, weight_sum), "expgrp")
    return flux_total / jnp.maximum(weight_total, 1.0)


def route(groups, owners, image, *rest):
    rows, columns = image.shape
    fits = rows == NB * BLK and columns == LANES * groups and BLK == 4 * owners and groups % 2 == 0
    return on_device_kernel(image, *rest) if fits else on_device(image, *rest)


def solution(mesh):
    in_specs = (
        P(("expgrp", "patch"), None),
        P(("expgrp", "patch"), None),
        P("expgrp", None),
        P("expgrp", None),
        P("expgrp"),
        P(),
    )
    out_specs = P("patch", None)
    return jax.shard_map(
        functools.partial(route, mesh.shape["expgrp"], mesh.shape["patch"]),
        mesh=mesh, in_specs=in_specs, out_specs=out_specs, check_vma=False,
    )
```

```python
import functools
import math

import jax
import jax.numpy as jnp
import numpy as np
from jax import lax
from jax.experimental import pallas as pl
from jax.experimental.pallas import tpu as pltpu
from jax.sharding import PartitionSpec as P

BLK = 16
CAP = 2
NS = 16
KH = 10
NB = 4
LANES = 128
SIDE = 64
EARLY = (((2, 0), (1, 0), (0, 1)), ((2, 0), (0, 0), (1, 1)), ((0, 0), (1, 0), (2, 1)), ((0, 0), (1, 0), (2, 0), (3, 1)))
ORDER = (((2, 0), (3, 0), (0, 1), (1, 0)), ((2, 0), (3, 0), (1, 1), (0, 0)), ((1, 0), (0, 0), (2, 1), (3, 0)), ((1, 0), (0, 0), (3, 1), (2, 0)))
SENDS = ((((2,), (1,)), ((2,), (3,), (0,)), ((1,), (0,), (3,)), ((1,), (2,))), (((1,), (2,), (3,)), ((2,), (3,), (0,)), ((3,), (0,), (1,)), ((0,), (1,), (2,))))
TAKES = ((((1, None), (2, None), (3, None)), ((2, None), (0, None), (3, 0)), ((3, None), (1, None), (0, 3)), ((2, None), (1, None), (0, None))), (((1, None), (2, None), (3, None)), ((2, None), (0, None), (3, None)), ((3, None), (1, None), (0, None)), ((2, None), (1, None), (0, None))))
COUNTS = ((((2,),), ((3,),), ((3,),), ((2,),)), (((3,),), ((3,),), ((3,),), ((3,),)))
PASSES = (((), ((3, 0),), ((0, 3),), ()), ((), (), (), ()))


SIGMAS = (0.75, 1.5, 3.0)
BASES = len(SIGMAS)
highest = lax.Precision.HIGHEST
MESH = pl.DeviceIdType.MESH


def np_profile(offsets, deviation):
    every = np.arange(-KH, KH + 1, dtype=np.float64)
    total = np.sum(np.exp(-every * every / (2.0 * deviation * deviation)))
    spacing = offsets.astype(np.float64)
    return np.where(
        np.abs(offsets) <= KH, np.exp(-spacing * spacing / (2.0 * deviation * deviation)) / total, 0.0
    ).astype(np.float32)


def np_row_table():
    row = np.arange(BLK * NB)
    r, n = row // NB, row % NB
    m, k = row // BLK, row % BLK
    same = (n[:, None] == m[None, :]).astype(np.float32)
    return np.concatenate([same * np_profile(k[None, :] - r[:, None], s) for s in SIGMAS], axis=0)


def np_column_table():
    i = np.arange(LANES + 2 * SIDE)[:, None]
    c = np.arange(LANES)[None, :]
    whole = np.concatenate([np_profile(i - SIDE - c, s) for s in SIGMAS], axis=0)
    high = whole.astype(jnp.bfloat16)
    low = (whole - high.astype(np.float32)).astype(jnp.bfloat16)
    return np.concatenate([high, low], axis=1)


def halves(x):
    high = x.astype(jnp.bfloat16)
    return high, (x - high.astype(jnp.float32)).astype(jnp.bfloat16)


def dot(a, b):
    return jnp.dot(a, b, preferred_element_type=jnp.float32)


def kernel(groups, owners, *refs):
    inputs, out, stage = refs[:8], refs[8], refs[9:17]
    (xpad, vbuf, both, dsrc, arrived, rd, cbuf,
     sb, qb, sd, qd, so, qo, sr, sx, qx, above, local, fetch) = refs[17:]
    loads = [pltpu.make_async_copy(a, b, fetch.at[n]) for n, (a, b) in enumerate(zip(inputs, stage))]
    for n in (1, 2, 3, 0, 4, 5, 6, 7):
        loads[n].start()
    img, var, count, start, psf, coef, rows_t, cols_t = stage
    g, p = lax.axis_index("expgrp"), lax.axis_index("patch")
    devices = groups * owners
    me = g * owners + p
    columns = img.shape[1]
    tiles = columns // LANES
    chips = groups // 2
    plane = 2 * owners
    z, core = g // 2, g % 2
    last = devices - plane
    late = z == chips - 1
    known = jnp.where(late, devices, last)

    def place_of(k):
        return (k // owners, lax.rem(k, owners))

    barrier = pltpu.get_barrier_semaphore()

    @pl.loop(1, jnp.where(late, plane, devices))
    def _(s):
        k = jnp.where(late, last + lax.rem(me - last + s, plane), lax.rem(me + s, devices))
        pl.semaphore_signal(barrier, inc=1, device_id=place_of(k), device_id_type=MESH)

    loads[2].wait()
    loads[3].wait()
    lane = lax.broadcasted_iota(jnp.int32, (1, LANES), 1)
    place = jnp.zeros((1, LANES), jnp.int32)
    block = lax.rem(lane, NB)
    for e in range(owners):
        first = jnp.int32(0)
        for q in range(owners):
            n_here = count[e, q]
            base = q * NS + start[e, q] - first
            inside = (lane // 8 == e) & (block >= first) & (block < first + n_here)
            place = jnp.where(inside, base + block, place)
            first = first + n_here
    dsrc[0] = place
    rd[g] = place
    loads[1].wait()

    for t in range(tiles):
        vbuf[t] = 1.0 / var[:, t * LANES:(t + 1) * LANES]
        for r in range(BLK):
            h, i = r // 8, (r // 2) % 4
            both[h, t * owners + i, 1, (r % 2) * NB:(r % 2) * NB + NB, :] = vbuf[t, pl.ds(r, NB, stride=BLK), :]

    def send(src, dst, ssem, rsem, k):
        return pltpu.make_async_remote_copy(
            src_ref=src, dst_ref=dst, send_sem=ssem, recv_sem=rsem,
            device_id=place_of(k), device_id_type=MESH,
        )

    def wait_for(ref, sem):
        pltpu.make_async_copy(ref, ref, sem).wait()

    def send_d(k):
        send(dsrc, rd.at[pl.ds(g, 1)], sd, qd, k).start()

    def send_b(h, k):
        send(both.at[h, k], arrived.at[h, me], sb.at[h], qb.at[h], k).start()

    def on_plane(table, act):
        for zz, entries in enumerate(table):
            if entries:
                @pl.when(z == zz)
                def _(entries=entries):
                    for entry in entries:
                        act(*entry)

    def to_planes(table, act):
        def to_plane(there, first):
            @pl.loop(first, plane)
            def _(s):
                act(plane * there + (lax.rem(me, plane) ^ s))

        on_plane(table, to_plane)

    xpad[:, :LANES] = jnp.zeros((NB * BLK, LANES), jnp.float32)
    xpad[:, columns:] = jnp.zeros((NB * BLK, LANES), jnp.float32)
    loads[0].wait()
    xpad[:, SIDE:SIDE + columns] = img[...]
    xh, xl = halves(xpad[...])
    for n in (4, 5, 6):
        loads[n].wait()
    which = psf[p]
    loads[7].wait()
    rows, part = NB * BLK, NB * BLK // 2
    wide = LANES + 2 * SIDE

    def smooth(h):
        ah, al = halves(jnp.concatenate(
            [rows_t[b * rows + h * part:b * rows + (h + 1) * part, :] * coef[b, which] for b in range(BASES)], axis=0
        ))
        yh, yl = halves(dot(ah, xh) + dot(al, xh) + dot(ah, xl))
        double = jnp.zeros((tiles * part, 2 * LANES), jnp.float32)
        one = jnp.zeros((tiles * part, LANES), jnp.float32)
        for b in range(BASES):
            def windows(y):
                return jnp.concatenate(
                    [y[b * part:(b + 1) * part, t * LANES:t * LANES + wide] for t in range(tiles)], axis=0
                )
            double = double + dot(windows(yh), cols_t[b * wide:(b + 1) * wide, :])
            one = one + dot(windows(yl), cols_t[b * wide:(b + 1) * wide, :LANES])
        total = double[:, :LANES] + double[:, LANES:] + one
        for t in range(tiles):
            for i in range(owners):
                k, at = t * owners + i, t * part + i * 8
                both[h, k, 0] = both[h, k, 1] * total[at:at + 8]

    smooth(0)
    pl.semaphore_wait(barrier, known - 1)

    @pl.when(late)
    def _():
        @pl.loop(0, last)
        def _(k):
            pl.semaphore_signal(above, inc=1, device_id=place_of(k), device_id_type=MESH)

    @pl.loop(1, known // owners)
    def _(s):
        send_d(lax.rem(g + s, known // owners) * owners + p)

    own = [pltpu.make_async_copy(both.at[h, me], arrived.at[h, me], local.at[h]) for h in range(2)]
    to_planes(EARLY, functools.partial(send_b, 0))
    own[0].start()
    smooth(1)

    @pl.when(z < chips - 1)
    def _():
        pl.semaphore_wait(above, plane)

        @pl.loop(0, 2)
        def _(c):
            send_d((groups - 2 + c) * owners + p)

        @pl.loop(0, plane)
        def _(s):
            send_b(0, last + lax.rem(me + s, plane))

    to_planes(ORDER, functools.partial(send_b, 1))
    own[1].start()

    wait_for(rd.at[pl.ds(0, groups - 1)], qd)

    many = devices * 8
    k_lane = lax.broadcasted_iota(jnp.int32, (1, many), 1)
    goal = jnp.zeros((1, many), jnp.int32)
    run = 8 * owners
    for h in range(groups):
        turned = pltpu.roll(rd[h], (h * run) % LANES, 1)
        goal = jnp.where(k_lane // run == h, jnp.concatenate([turned] * (many // LANES), axis=1), goal)
    slots = owners * NS
    goal = goal + slots * lax.rem(k_lane // NB, 2)
    row = lax.broadcasted_iota(jnp.int32, (2 * slots, many), 0)
    hot = jnp.where(row == goal, 1.0, 0.0).astype(jnp.bfloat16)

    def piece(h, there, q):
        k = (2 * there + core) * owners + q
        return send(cbuf.at[h, q], out.at[h, g, p], so.at[h], qo.at[h, z], k)

    own_o = [pltpu.make_async_copy(cbuf.at[h, p], out.at[h, g, p], local.at[2 + h]) for h in range(2)]

    def each_piece(h, act):
        def to_plane(there):
            for v in range(owners):
                act(piece(h, there, lax.rem(p + v, owners)))

        on_plane(SENDS[h], to_plane)
        for v in range(1, owners):
            act(piece(h, z, lax.rem(p + v, owners)))

    def add_up(h):
        wait_for(arrived.at[h, pl.ds(0, devices - 1)], qb.at[h])
        own[h].wait()
        high, low_part = halves(jnp.concatenate([arrived[h, :, n].reshape(many, LANES) for n in range(2)], axis=1))
        total = dot(hot, high) + dot(hot, low_part)
        ratio = total[:, :LANES] / jnp.maximum(total[:, LANES:], 1.0)
        for q in range(owners):
            for r2 in range(2):
                cbuf[h, q, r2] = ratio[r2 * slots + q * NS:r2 * slots + (q + 1) * NS]
        each_piece(h, lambda copy: copy.start())
        own_o[h].start()

    sibling = (z * 2 + 1 - core) * owners + p

    def across(h, there, side):
        j = there * 2 + side
        return send(out.at[h, j], out.at[h, j], sx.at[h], qx.at[h], sibling)

    def onward(h, there, to):
        j = there * 2 + core
        return send(out.at[h, j], out.at[h, j], sr.at[h, there], qo.at[h, there], (to * 2 + core) * owners + p)

    def take(h, there, to):
        wait_for(out.at[h, there * 2 + core], qo.at[h, there])
        if to is not None:
            onward(h, there, to).start()
        across(h, there, core).start()

    def relay(h):
        wait_for(out.at[h, g, pl.ds(0, owners - 1)], qo.at[h, z])
        own_o[h].wait()
        across(h, z, core).start()
        on_plane(TAKES[h], functools.partial(take, h))

    def drain(h):
        on_plane(COUNTS[h], lambda n: wait_for(out.at[h, pl.ds(0, n)], so.at[h]))
        wait_for(out.at[h, 0, pl.ds(0, owners - 1)], so.at[h])
        on_plane(PASSES[h], lambda there, to: onward(h, there, to).wait_send())

    add_up(0)
    add_up(1)
    wait_for(rd.at[pl.ds(0, groups - 1)], sd)
    for h in range(2):
        wait_for(arrived.at[h, pl.ds(0, devices - 1)], sb.at[h])
    relay(0)
    drain(0)
    relay(1)
    drain(1)
    for sem in (qx, sx):
        for h in range(2):
            wait_for(out.at[h, pl.ds(0, chips)], sem.at[h])


def lay_out(parts, out, flat, sem):
    copies = []
    for t in range(flat.shape[0]):
        at = slice(t * LANES, (t + 1) * LANES)
        for h in range(2):
            for i in range(BLK // 4):
                for r2 in range(2):
                    flat[t, pl.ds(h * 8 + i * 2 + r2, NS, stride=BLK), :] = parts[h, t, i, r2]
        copy = pltpu.make_async_copy(flat.at[t], out.at[:, at], sem.at[t])
        copy.start()
        copies.append(copy)
    for copy in copies:
        copy.wait()


def on_device_kernel(image, variance, block_count, slot_start, psf_index, coef_table):
    groups, owners = lax.axis_size("expgrp"), lax.axis_size("patch")
    devices = groups * owners
    rows, columns = image.shape
    slots = owners * NS
    dma = pltpu.SemaphoreType.DMA
    f32 = jnp.float32
    hbm = pl.BlockSpec(memory_space=pltpu.HBM)
    parts = pl.pallas_call(
        functools.partial(kernel, groups, owners),
        out_shape=pltpu.VMEM((2, groups, owners, 2, NS, LANES), f32),
        in_specs=[hbm] * 8,
        out_specs=pl.BlockSpec(memory_space=pl.ANY),
        scratch_shapes=[
            pltpu.VMEM((rows, columns), f32),
            pltpu.VMEM((rows, columns), f32),
            pltpu.SMEM(block_count.shape, jnp.int32),
            pltpu.SMEM(slot_start.shape, jnp.int32),
            pltpu.SMEM(psf_index.shape, jnp.int32),
            pltpu.SMEM(coef_table.shape[::-1], f32),
            pltpu.VMEM((BASES * rows, rows), f32),
            pltpu.VMEM((BASES * (LANES + 2 * SIDE), 2 * LANES), jnp.bfloat16),
            pltpu.VMEM((rows, columns + 2 * SIDE), f32),
            pltpu.VMEM((columns // LANES, rows, LANES), f32),
            pltpu.VMEM((2, devices, 2, 8, LANES), f32),
            pltpu.VMEM((1, 1, LANES), jnp.int32),
            pltpu.VMEM((2, devices, 2, 8, LANES), f32),
            pltpu.VMEM((groups, 1, LANES), jnp.int32),
            pltpu.VMEM((2, owners, 2, NS, LANES), f32),
            dma((2,)), dma((2,)), dma, dma,
            dma((2,)), dma((2, groups // 2)), dma((2, groups // 2)),
            dma((2,)), dma((2,)),
            pltpu.SemaphoreType.REGULAR,
            dma((4,)), dma((8,)),
        ],
        compiler_params=pltpu.CompilerParams(
            collective_id=0, has_side_effects=True, vmem_limit_bytes=56 * 1024 * 1024
        ),
    )(
        image, variance, block_count, slot_start, psf_index, coef_table.T,
        jnp.asarray(np_row_table()), jnp.asarray(np_column_table()),
    )
    return pl.pallas_call(
        lay_out,
        out_shape=jax.ShapeDtypeStruct((NS * BLK, columns), f32),
        in_specs=[pl.BlockSpec(memory_space=pltpu.VMEM)],
        out_specs=hbm,
        scratch_shapes=[pltpu.VMEM((columns // LANES, NS * BLK, LANES), f32), dma((columns // LANES,))],
        compiler_params=pltpu.CompilerParams(vmem_limit_bytes=16 * 1024 * 1024),
    )(parts)


def profile(offsets, deviation):
    offset_range = jnp.arange(-KH, KH + 1).astype(jnp.float32)
    total = jnp.sum(jnp.exp(-offset_range * offset_range / (2.0 * deviation * deviation)))
    spacing = offsets.astype(jnp.float32)
    return jnp.where(
        jnp.abs(offsets) <= KH,
        jnp.exp(-spacing * spacing / (2.0 * deviation * deviation)) / total,
        jnp.float32(0.0),
    )


def column_table(tile_width):
    inner_index = jnp.arange(3 * tile_width, dtype=jnp.int32)[:, None]
    outer_index = jnp.arange(tile_width, dtype=jnp.int32)[None, :]
    columns_list = [
        profile(inner_index - tile_width - outer_index, deviation) for deviation in SIGMAS
    ]
    return jnp.concatenate(columns_list, axis=1)


def row_table(height):
    row_index = jnp.arange(height, dtype=jnp.int32)
    return jnp.stack(
        [profile(row_index[None, :] - row_index[:, None], deviation) for deviation in SIGMAS]
    )


def matched(blocks, mixing):
    number, height, columns = blocks.shape
    tile_width = 128
    tile_count = columns // tile_width
    parted = blocks.reshape(number, height, tile_count, tile_width)
    blank = jnp.zeros((number, height, 1, tile_width), jnp.float32)
    behind = jnp.concatenate([blank, parted[:, :, :-1]], axis=2)
    follow = jnp.concatenate([parted[:, :, 1:], blank], axis=2)
    joined = jnp.concatenate([behind, parted, follow], axis=3)
    across = jnp.einsum("nrti,ik->nrtk", joined, column_table(tile_width), precision=highest)
    across = across.reshape(number, height, tile_count, len(SIGMAS), tile_width)
    vertical = mixing[:, :, None, None] * row_table(height)[None]
    result = jnp.einsum("nbrk,nktbc->nrtc", vertical, across, precision=highest)
    return result.reshape(number, height, columns)


def on_device(image, variance, block_count, slot_start, psf_index, coef_table):
    owners = lax.axis_size("patch")
    own_index = lax.axis_index("patch")
    tile_rows, columns = image.shape
    number = tile_rows // BLK
    lookup = (
        jnp.arange(coef_table.shape[0], dtype=jnp.int32)[None, :] == psf_index[:, None]
    ).astype(jnp.float32)
    mixing = jnp.sum(lookup[:, :, None] * coef_table[None, :, :], axis=1)
    own_count = lax.dynamic_index_in_dim(block_count, own_index, 0, keepdims=False)
    before = jnp.arange(owners)[None, :] < jnp.arange(owners)[:, None]
    firsts = jnp.sum(jnp.where(before, own_count[None, :], 0), axis=1)
    places = jnp.arange(CAP, dtype=jnp.int32)
    source = firsts[:, None] + places[None, :]
    filled = places[None, :] < own_count[:, None]

    def arrange(values):
        total = jnp.zeros((owners, CAP, BLK, columns), jnp.float32)
        for n in range(number):
            here = (source == n) & filled
            total = jnp.where(here[:, :, None, None], values[n][None, None], total)
        return total

    image_blocks = image.reshape(number, BLK, columns)
    scale_blocks = variance.reshape(number, BLK, columns)
    raw_blocks = lax.all_to_all(
        arrange(image_blocks), "patch", split_axis=0, concat_axis=0, tiled=True
    )
    raw_scales = lax.all_to_all(
        arrange(scale_blocks), "patch", split_axis=0, concat_axis=0, tiled=True
    )
    senders = raw_blocks.shape[0]
    slot_count = raw_blocks.shape[1]
    present = raw_scales > 0.0
    weights = jnp.where(present, 1.0 / jnp.where(present, raw_scales, 1.0), 0.0)
    spread = jnp.broadcast_to(mixing[:, None, :], (senders, slot_count, mixing.shape[1]))
    smooth = matched(
        raw_blocks.reshape(senders * slot_count, BLK, columns),
        spread.reshape(senders * slot_count, mixing.shape[1]),
    )
    arrived_flux = weights * smooth.reshape(raw_blocks.shape)
    arrived_count = lax.dynamic_index_in_dim(block_count, own_index, 1, keepdims=False)
    arrived_start = lax.dynamic_index_in_dim(slot_start, own_index, 1, keepdims=False)
    slots = jnp.arange(NS, dtype=jnp.int32)
    target = (places[None, :] < arrived_count[:, None])[None] & (
        arrived_start[:, None] + places[None, :] == slots[:, None, None]
    )
    layout = target.astype(jnp.float32)
    flux_sum = jnp.einsum("spj,pjrw->srw", layout, arrived_flux, precision=highest).reshape(
        NS * BLK, columns
    )
    weight_sum = jnp.einsum("spj,pjrw->srw", layout, weights, precision=highest).reshape(
        NS * BLK, columns
    )
    flux_total, weight_total = lax.psum((flux_sum, weight_sum), "expgrp")
    return flux_total / jnp.maximum(weight_total, 1.0)


def route(groups, owners, image, *rest):
    rows, columns = image.shape
    fits = rows == NB * BLK and columns == LANES * groups and BLK == 4 * owners and groups % 2 == 0
    return on_device_kernel(image, *rest) if fits else on_device(image, *rest)


def solution(mesh):
    in_specs = (
        P(("expgrp", "patch"), None),
        P(("expgrp", "patch"), None),
        P("expgrp", None),
        P("expgrp", None),
        P("expgrp"),
        P(),
    )
    out_specs = P("patch", None)
    return jax.shard_map(
        functools.partial(route, mesh.shape["expgrp"], mesh.shape["patch"]),
        mesh=mesh, in_specs=in_specs, out_specs=out_specs, check_vma=False,
    )
```

```python
import functools
import math

import jax
import jax.numpy as jnp
import numpy as np
from jax import lax
from jax.experimental import pallas as pl
from jax.experimental.pallas import tpu as pltpu
from jax.sharding import PartitionSpec as P

BLK = 16
CAP = 2
NS = 16
KH = 10
NB = 4
LANES = 128
SIDE = 64
EARLY = (((2, 0), (1, 0), (0, 1)), ((2, 0), (0, 0), (1, 1)), ((0, 0), (1, 0), (2, 1)), ((0, 0), (1, 0), (2, 0), (3, 1)))
ORDER = (((2, 0), (3, 0), (0, 1), (1, 0)), ((2, 0), (3, 0), (1, 1), (0, 0)), ((1, 0), (0, 0), (2, 1), (3, 0)), ((1, 0), (0, 0), (3, 1), (2, 0)))
SENDS = ((((2,), (1,)), ((2,), (3,), (0,)), ((1,), (0,), (3,)), ((1,), (2,))), (((1,), (2,), (3,)), ((2,), (3,), (0,)), ((3,), (0,), (1,)), ((0,), (1,), (2,))))
TAKES = ((((1, None), (2, None), (3, None)), ((2, None), (0, None), (3, 0)), ((3, None), (1, None), (0, 3)), ((2, None), (1, None), (0, None))), (((1, None), (2, None), (3, None)), ((2, None), (0, None), (3, None)), ((3, None), (1, None), (0, None)), ((2, None), (1, None), (0, None))))
COUNTS = ((((2,),), ((3,),), ((3,),), ((2,),)), (((3,),), ((3,),), ((3,),), ((3,),)))
PASSES = (((), ((3, 0),), ((0, 3),), ()), ((), (), (), ()))


SIGMAS = (0.75, 1.5, 3.0)
BASES = len(SIGMAS)
highest = lax.Precision.HIGHEST
MESH = pl.DeviceIdType.MESH


def np_profile(offsets, deviation):
    every = np.arange(-KH, KH + 1, dtype=np.float64)
    total = np.sum(np.exp(-every * every / (2.0 * deviation * deviation)))
    spacing = offsets.astype(np.float64)
    return np.where(
        np.abs(offsets) <= KH, np.exp(-spacing * spacing / (2.0 * deviation * deviation)) / total, 0.0
    ).astype(np.float32)


def np_row_table():
    row = np.arange(BLK * NB)
    r, n = row // NB, row % NB
    m, k = row // BLK, row % BLK
    same = (n[:, None] == m[None, :]).astype(np.float32)
    return np.concatenate([same * np_profile(k[None, :] - r[:, None], s) for s in SIGMAS], axis=0)


def np_column_table():
    i = np.arange(LANES + 2 * SIDE)[:, None]
    c = np.arange(LANES)[None, :]
    whole = np.concatenate([np_profile(i - SIDE - c, s) for s in SIGMAS], axis=0)
    high = whole.astype(jnp.bfloat16)
    low = (whole - high.astype(np.float32)).astype(jnp.bfloat16)
    return np.concatenate([high, low], axis=1)


def halves(x):
    high = x.astype(jnp.bfloat16)
    return high, (x - high.astype(jnp.float32)).astype(jnp.bfloat16)


def dot(a, b):
    return jnp.dot(a, b, preferred_element_type=jnp.float32)


def kernel(groups, owners, *refs):
    inputs, out, stage = refs[:8], refs[8], refs[9:17]
    (xpad, vbuf, both, dsrc, arrived, rd, cbuf,
     sb, qb, sd, qd, so, qo, sr, sx, qx, above, local, fetch) = refs[17:]
    loads = [pltpu.make_async_copy(a, b, fetch.at[n]) for n, (a, b) in enumerate(zip(inputs, stage))]
    for n in (1, 2, 3, 0, 4, 5, 6, 7):
        loads[n].start()
    img, var, count, start, psf, coef, rows_t, cols_t = stage
    g, p = lax.axis_index("expgrp"), lax.axis_index("patch")
    devices = groups * owners
    me = g * owners + p
    columns = img.shape[1]
    tiles = columns // LANES
    chips = groups // 2
    plane = 2 * owners
    z, core = g // 2, g % 2
    last = devices - plane
    late = z == chips - 1
    known = jnp.where(late, devices, last)

    def place_of(k):
        return (k // owners, lax.rem(k, owners))

    barrier = pltpu.get_barrier_semaphore()

    @pl.loop(1, jnp.where(late, plane, devices))
    def _(s):
        k = jnp.where(late, last + lax.rem(me - last + s, plane), lax.rem(me + s, devices))
        pl.semaphore_signal(barrier, inc=1, device_id=place_of(k), device_id_type=MESH)

    loads[2].wait()
    loads[3].wait()
    lane = lax.broadcasted_iota(jnp.int32, (1, LANES), 1)
    place = jnp.zeros((1, LANES), jnp.int32)
    block = lax.rem(lane, NB)
    for e in range(owners):
        first = jnp.int32(0)
        for q in range(owners):
            n_here = count[e, q]
            base = q * NS + start[e, q] - first
            inside = (lane // 8 == e) & (block >= first) & (block < first + n_here)
            place = jnp.where(inside, base + block, place)
            first = first + n_here
    dsrc[0] = place
    rd[g] = place
    loads[1].wait()

    for t in range(tiles):
        vbuf[t] = 1.0 / var[:, t * LANES:(t + 1) * LANES]
        for r in range(BLK):
            h, i = r // 8, (r // 2) % 4
            both[h, t * owners + i, 1, (r % 2) * NB:(r % 2) * NB + NB, :] = vbuf[t, pl.ds(r, NB, stride=BLK), :]

    def send(src, dst, ssem, rsem, k):
        return pltpu.make_async_remote_copy(
            src_ref=src, dst_ref=dst, send_sem=ssem, recv_sem=rsem,
            device_id=place_of(k), device_id_type=MESH,
        )

    def wait_for(ref, sem):
        pltpu.make_async_copy(ref, ref, sem).wait()

    def send_d(k):
        send(dsrc, rd.at[pl.ds(g, 1)], sd, qd, k).start()

    def send_b(h, k):
        send(both.at[h, k], arrived.at[h, me], sb.at[h], qb.at[h], k).start()

    def on_plane(table, act):
        for zz, entries in enumerate(table):
            if entries:
                @pl.when(z == zz)
                def _(entries=entries):
                    for entry in entries:
                        act(*entry)

    def to_planes(table, act):
        def to_plane(there, first):
            @pl.loop(first, plane)
            def _(s):
                act(plane * there + (lax.rem(me, plane) ^ s))

        on_plane(table, to_plane)

    xpad[:, :LANES] = jnp.zeros((NB * BLK, LANES), jnp.float32)
    xpad[:, columns:] = jnp.zeros((NB * BLK, LANES), jnp.float32)
    loads[0].wait()
    xpad[:, SIDE:SIDE + columns] = img[...]
    xh, xl = halves(xpad[...])
    for n in (4, 5, 6):
        loads[n].wait()
    which = psf[p]
    loads[7].wait()
    rows, part = NB * BLK, NB * BLK // 2
    wide = LANES + 2 * SIDE

    def smooth(h):
        ah, al = halves(jnp.concatenate(
            [rows_t[b * rows + h * part:b * rows + (h + 1) * part, :] * coef[b, which] for b in range(BASES)], axis=0
        ))
        yh, yl = halves(dot(ah, xh) + dot(al, xh) + dot(ah, xl))
        double = jnp.zeros((tiles * part, 2 * LANES), jnp.float32)
        one = jnp.zeros((tiles * part, LANES), jnp.float32)
        for b in range(BASES):
            def windows(y):
                return jnp.concatenate(
                    [y[b * part:(b + 1) * part, t * LANES:t * LANES + wide] for t in range(tiles)], axis=0
                )
            double = double + dot(windows(yh), cols_t[b * wide:(b + 1) * wide, :])
            one = one + dot(windows(yl), cols_t[b * wide:(b + 1) * wide, :LANES])
        total = double[:, :LANES] + double[:, LANES:] + one
        for t in range(tiles):
            for i in range(owners):
                k, at = t * owners + i, t * part + i * 8
                both[h, k, 0] = both[h, k, 1] * total[at:at + 8]

    smooth(0)
    pl.semaphore_wait(barrier, known - 1)

    @pl.when(late)
    def _():
        @pl.loop(0, last)
        def _(k):
            pl.semaphore_signal(above, inc=1, device_id=place_of(k), device_id_type=MESH)

    @pl.loop(1, known // owners)
    def _(s):
        send_d(lax.rem(g + s, known // owners) * owners + p)

    own = [pltpu.make_async_copy(both.at[h, me], arrived.at[h, me], local.at[h]) for h in range(2)]
    to_planes(EARLY, functools.partial(send_b, 0))
    own[0].start()
    @pl.when(z < chips - 1)
    def _():
        pl.semaphore_wait(above, plane)

        @pl.loop(0, 2)
        def _(c):
            send_d((groups - 2 + c) * owners + p)

        @pl.loop(0, plane)
        def _(s):
            send_b(0, last + lax.rem(me + s, plane))

    smooth(1)
    to_planes(ORDER, functools.partial(send_b, 1))
    own[1].start()

    wait_for(rd.at[pl.ds(0, groups - 1)], qd)

    many = devices * 8
    k_lane = lax.broadcasted_iota(jnp.int32, (1, many), 1)
    goal = jnp.zeros((1, many), jnp.int32)
    run = 8 * owners
    for h in range(groups):
        turned = pltpu.roll(rd[h], (h * run) % LANES, 1)
        goal = jnp.where(k_lane // run == h, jnp.concatenate([turned] * (many // LANES), axis=1), goal)
    slots = owners * NS
    goal = goal + slots * lax.rem(k_lane // NB, 2)
    row = lax.broadcasted_iota(jnp.int32, (2 * slots, many), 0)
    hot = jnp.where(row == goal, 1.0, 0.0).astype(jnp.bfloat16)

    def piece(h, there, q):
        k = (2 * there + core) * owners + q
        return send(cbuf.at[h, q], out.at[h, g, p], so.at[h], qo.at[h, z], k)

    own_o = [pltpu.make_async_copy(cbuf.at[h, p], out.at[h, g, p], local.at[2 + h]) for h in range(2)]

    def each_piece(h, act):
        def to_plane(there):
            for v in range(owners):
                act(piece(h, there, lax.rem(p + v, owners)))

        for v in range(1, owners):
            act(piece(h, z, lax.rem(p + v, owners)))
        on_plane(SENDS[h], to_plane)

    def add_up(h):
        wait_for(arrived.at[h, pl.ds(0, devices - 1)], qb.at[h])
        own[h].wait()
        high, low_part = halves(jnp.concatenate([arrived[h, :, n].reshape(many, LANES) for n in range(2)], axis=1))
        total = dot(hot, high) + dot(hot, low_part)
        ratio = total[:, :LANES] / jnp.maximum(total[:, LANES:], 1.0)
        for q in range(owners):
            for r2 in range(2):
                cbuf[h, q, r2] = ratio[r2 * slots + q * NS:r2 * slots + (q + 1) * NS]
        each_piece(h, lambda copy: copy.start())
        own_o[h].start()

    sibling = (z * 2 + 1 - core) * owners + p

    def across(h, there, side):
        j = there * 2 + side
        return send(out.at[h, j], out.at[h, j], sx.at[h], qx.at[h], sibling)

    def onward(h, there, to):
        j = there * 2 + core
        return send(out.at[h, j], out.at[h, j], sr.at[h, there], qo.at[h, there], (to * 2 + core) * owners + p)

    def take(h, there, to):
        wait_for(out.at[h, there * 2 + core], qo.at[h, there])
        if to is not None:
            onward(h, there, to).start()
        across(h, there, core).start()

    def relay(h):
        wait_for(out.at[h, g, pl.ds(0, owners - 1)], qo.at[h, z])
        own_o[h].wait()
        across(h, z, core).start()
        on_plane(TAKES[h], functools.partial(take, h))

    def drain(h):
        on_plane(COUNTS[h], lambda n: wait_for(out.at[h, pl.ds(0, n)], so.at[h]))
        wait_for(out.at[h, 0, pl.ds(0, owners - 1)], so.at[h])
        on_plane(PASSES[h], lambda there, to: onward(h, there, to).wait_send())

    add_up(0)
    add_up(1)
    wait_for(rd.at[pl.ds(0, groups - 1)], sd)
    for h in range(2):
        wait_for(arrived.at[h, pl.ds(0, devices - 1)], sb.at[h])
    relay(0)
    drain(0)
    relay(1)
    drain(1)
    for sem in (qx, sx):
        for h in range(2):
            wait_for(out.at[h, pl.ds(0, chips)], sem.at[h])


def lay_out(parts, out, flat, sem):
    copies = []
    for t in range(flat.shape[0]):
        at = slice(t * LANES, (t + 1) * LANES)
        for h in range(2):
            for i in range(BLK // 4):
                for r2 in range(2):
                    flat[t, pl.ds(h * 8 + i * 2 + r2, NS, stride=BLK), :] = parts[h, t, i, r2]
        copy = pltpu.make_async_copy(flat.at[t], out.at[:, at], sem.at[t])
        copy.start()
        copies.append(copy)
    for copy in copies:
        copy.wait()


def on_device_kernel(image, variance, block_count, slot_start, psf_index, coef_table):
    groups, owners = lax.axis_size("expgrp"), lax.axis_size("patch")
    devices = groups * owners
    rows, columns = image.shape
    slots = owners * NS
    dma = pltpu.SemaphoreType.DMA
    f32 = jnp.float32
    hbm = pl.BlockSpec(memory_space=pltpu.HBM)
    parts = pl.pallas_call(
        functools.partial(kernel, groups, owners),
        out_shape=pltpu.VMEM((2, groups, owners, 2, NS, LANES), f32),
        in_specs=[hbm] * 8,
        out_specs=pl.BlockSpec(memory_space=pl.ANY),
        scratch_shapes=[
            pltpu.VMEM((rows, columns), f32),
            pltpu.VMEM((rows, columns), f32),
            pltpu.SMEM(block_count.shape, jnp.int32),
            pltpu.SMEM(slot_start.shape, jnp.int32),
            pltpu.SMEM(psf_index.shape, jnp.int32),
            pltpu.SMEM(coef_table.shape[::-1], f32),
            pltpu.VMEM((BASES * rows, rows), f32),
            pltpu.VMEM((BASES * (LANES + 2 * SIDE), 2 * LANES), jnp.bfloat16),
            pltpu.VMEM((rows, columns + 2 * SIDE), f32),
            pltpu.VMEM((columns // LANES, rows, LANES), f32),
            pltpu.VMEM((2, devices, 2, 8, LANES), f32),
            pltpu.VMEM((1, 1, LANES), jnp.int32),
            pltpu.VMEM((2, devices, 2, 8, LANES), f32),
            pltpu.VMEM((groups, 1, LANES), jnp.int32),
            pltpu.VMEM((2, owners, 2, NS, LANES), f32),
            dma((2,)), dma((2,)), dma, dma,
            dma((2,)), dma((2, groups // 2)), dma((2, groups // 2)),
            dma((2,)), dma((2,)),
            pltpu.SemaphoreType.REGULAR,
            dma((4,)), dma((8,)),
        ],
        compiler_params=pltpu.CompilerParams(
            collective_id=0, has_side_effects=True, vmem_limit_bytes=56 * 1024 * 1024
        ),
    )(
        image, variance, block_count, slot_start, psf_index, coef_table.T,
        jnp.asarray(np_row_table()), jnp.asarray(np_column_table()),
    )
    return pl.pallas_call(
        lay_out,
        out_shape=jax.ShapeDtypeStruct((NS * BLK, columns), f32),
        in_specs=[pl.BlockSpec(memory_space=pltpu.VMEM)],
        out_specs=hbm,
        scratch_shapes=[pltpu.VMEM((columns // LANES, NS * BLK, LANES), f32), dma((columns // LANES,))],
        compiler_params=pltpu.CompilerParams(vmem_limit_bytes=16 * 1024 * 1024),
    )(parts)


def profile(offsets, deviation):
    offset_range = jnp.arange(-KH, KH + 1).astype(jnp.float32)
    total = jnp.sum(jnp.exp(-offset_range * offset_range / (2.0 * deviation * deviation)))
    spacing = offsets.astype(jnp.float32)
    return jnp.where(
        jnp.abs(offsets) <= KH,
        jnp.exp(-spacing * spacing / (2.0 * deviation * deviation)) / total,
        jnp.float32(0.0),
    )


def column_table(tile_width):
    inner_index = jnp.arange(3 * tile_width, dtype=jnp.int32)[:, None]
    outer_index = jnp.arange(tile_width, dtype=jnp.int32)[None, :]
    columns_list = [
        profile(inner_index - tile_width - outer_index, deviation) for deviation in SIGMAS
    ]
    return jnp.concatenate(columns_list, axis=1)


def row_table(height):
    row_index = jnp.arange(height, dtype=jnp.int32)
    return jnp.stack(
        [profile(row_index[None, :] - row_index[:, None], deviation) for deviation in SIGMAS]
    )


def matched(blocks, mixing):
    number, height, columns = blocks.shape
    tile_width = 128
    tile_count = columns // tile_width
    parted = blocks.reshape(number, height, tile_count, tile_width)
    blank = jnp.zeros((number, height, 1, tile_width), jnp.float32)
    behind = jnp.concatenate([blank, parted[:, :, :-1]], axis=2)
    follow = jnp.concatenate([parted[:, :, 1:], blank], axis=2)
    joined = jnp.concatenate([behind, parted, follow], axis=3)
    across = jnp.einsum("nrti,ik->nrtk", joined, column_table(tile_width), precision=highest)
    across = across.reshape(number, height, tile_count, len(SIGMAS), tile_width)
    vertical = mixing[:, :, None, None] * row_table(height)[None]
    result = jnp.einsum("nbrk,nktbc->nrtc", vertical, across, precision=highest)
    return result.reshape(number, height, columns)


def on_device(image, variance, block_count, slot_start, psf_index, coef_table):
    owners = lax.axis_size("patch")
    own_index = lax.axis_index("patch")
    tile_rows, columns = image.shape
    number = tile_rows // BLK
    lookup = (
        jnp.arange(coef_table.shape[0], dtype=jnp.int32)[None, :] == psf_index[:, None]
    ).astype(jnp.float32)
    mixing = jnp.sum(lookup[:, :, None] * coef_table[None, :, :], axis=1)
    own_count = lax.dynamic_index_in_dim(block_count, own_index, 0, keepdims=False)
    before = jnp.arange(owners)[None, :] < jnp.arange(owners)[:, None]
    firsts = jnp.sum(jnp.where(before, own_count[None, :], 0), axis=1)
    places = jnp.arange(CAP, dtype=jnp.int32)
    source = firsts[:, None] + places[None, :]
    filled = places[None, :] < own_count[:, None]

    def arrange(values):
        total = jnp.zeros((owners, CAP, BLK, columns), jnp.float32)
        for n in range(number):
            here = (source == n) & filled
            total = jnp.where(here[:, :, None, None], values[n][None, None], total)
        return total

    image_blocks = image.reshape(number, BLK, columns)
    scale_blocks = variance.reshape(number, BLK, columns)
    raw_blocks = lax.all_to_all(
        arrange(image_blocks), "patch", split_axis=0, concat_axis=0, tiled=True
    )
    raw_scales = lax.all_to_all(
        arrange(scale_blocks), "patch", split_axis=0, concat_axis=0, tiled=True
    )
    senders = raw_blocks.shape[0]
    slot_count = raw_blocks.shape[1]
    present = raw_scales > 0.0
    weights = jnp.where(present, 1.0 / jnp.where(present, raw_scales, 1.0), 0.0)
    spread = jnp.broadcast_to(mixing[:, None, :], (senders, slot_count, mixing.shape[1]))
    smooth = matched(
        raw_blocks.reshape(senders * slot_count, BLK, columns),
        spread.reshape(senders * slot_count, mixing.shape[1]),
    )
    arrived_flux = weights * smooth.reshape(raw_blocks.shape)
    arrived_count = lax.dynamic_index_in_dim(block_count, own_index, 1, keepdims=False)
    arrived_start = lax.dynamic_index_in_dim(slot_start, own_index, 1, keepdims=False)
    slots = jnp.arange(NS, dtype=jnp.int32)
    target = (places[None, :] < arrived_count[:, None])[None] & (
        arrived_start[:, None] + places[None, :] == slots[:, None, None]
    )
    layout = target.astype(jnp.float32)
    flux_sum = jnp.einsum("spj,pjrw->srw", layout, arrived_flux, precision=highest).reshape(
        NS * BLK, columns
    )
    weight_sum = jnp.einsum("spj,pjrw->srw", layout, weights, precision=highest).reshape(
        NS * BLK, columns
    )
    flux_total, weight_total = lax.psum((flux_sum, weight_sum), "expgrp")
    return flux_total / jnp.maximum(weight_total, 1.0)


def route(groups, owners, image, *rest):
    rows, columns = image.shape
    fits = rows == NB * BLK and columns == LANES * groups and BLK == 4 * owners and groups % 2 == 0
    return on_device_kernel(image, *rest) if fits else on_device(image, *rest)


def solution(mesh):
    in_specs = (
        P(("expgrp", "patch"), None),
        P(("expgrp", "patch"), None),
        P("expgrp", None),
        P("expgrp", None),
        P("expgrp"),
        P(),
    )
    out_specs = P("patch", None)
    return jax.shard_map(
        functools.partial(route, mesh.shape["expgrp"], mesh.shape["patch"]),
        mesh=mesh, in_specs=in_specs, out_specs=out_specs, check_vma=False,
    )
```
